128 devices in a mesh: ctx: 32 (over y, x, core), tp: 4 (over z).
Axes of the slice: x: 4, y: 4, z: 4, core: 2. Of those that a mesh axis runs over, the one named last changes fastest.
Arguments:
- hidden_in: bfloat16 [32, 4096], P('ctx', 'tp'), may hold values from -6 to 6
- query: bfloat16 [32, 4096], P('ctx', 'tp')
- new_key: bfloat16 [32, 1024], P('ctx', 'tp'), may hold values from -8 to 8
- new_value: bfloat16 [32, 1024], P('ctx', 'tp'), may hold values from -6 to 6
- cache_keys: bfloat16 [32, 16384, 1024], P(None, 'ctx', 'tp')
- cache_values: bfloat16 [32, 16384, 1024], P(None, 'ctx', 'tp'), may hold values from -6 to 6
- lengths: int32 [32], replicated, may hold values from 1 to 16384, as said below
- out_weight: bfloat16 [4096, 4096], P('tp', 'ctx'), may hold values from -0.09375 to 0.09375
- norm_gain: float32 [4096], P('tp'), may hold values from 0.1 to 1.9
- w_gate: bfloat16 [4096, 14336], P(None, ('ctx', 'tp')), may hold values from -0.09375 to 0.09375
- w_up: bfloat16 [4096, 14336], P(None, ('ctx', 'tp')), may hold values from -0.09375 to 0.09375
- w_down: bfloat16 [14336, 4096], P(('ctx', 'tp')), may hold values from -0.1875 to 0.1875
Outputs:
- layer_out: bfloat16 [32, 4096], P('ctx', 'tp')
The draws below stay inside these ranges and needn't reach their ends.
Inputs may be any that keep to these rules, and one draw needn't show every extreme that they name: Positions 0 to lengths[b] - 1 of sequence b hold its cached tokens; some sequence has all 16384 positions valid and another exactly one.
All inputs are finite; a program needn't handle non-finite values.
Results may differ from the reference program's by a relative error of at most 0.009.
Values may be sent and summed in bfloat16 or wider, within the bound.
No kernel may reach another device: no remote copies, remote signals or barrier semaphores. Data moves between devices by JAX's collectives and lax.ppermute only.
A program may use at most 64 MiB of HBM per device.

```python
import math
import jax
import jax.numpy as jnp
from jax import lax

D = 4096
H = 32
KVH = 8
HD = 128
FF = 14336
CTX_DEV = 512
SEQS = 32
CTX = 16384
N_CTX = 32


def lead_keys(key):
    return jnp.clip(jax.random.normal(key, (SEQS, KVH * HD), jnp.float32), -4.0, 4.0) * 2.0


def draw_cache_keys(key, part):
    first_rows = lead_keys(key)
    key = jax.random.fold_in(key, 5)
    later_rows = jnp.clip(jax.random.normal(key, (SEQS, CTX - 1, KVH * HD), jnp.float32), -4.0, 4.0) * 2.0
    return jnp.concatenate([first_rows[:, None], later_rows], axis=1).astype(jnp.bfloat16)


def draw_query(key, part):
    key = jax.random.fold_in(key, 3)
    random_part = jnp.clip(jax.random.normal(key, (SEQS, H * HD), jnp.float32), -6.0, 6.0)
    return random_part.astype(jnp.bfloat16)


def draw_lengths(key, part):
    key = jax.random.fold_in(key, 7)
    first_key, second_key, third_key = jax.random.split(key, 3)
    drawn = jax.random.randint(first_key, (SEQS,), 1, CTX + 1)
    longest = jax.random.randint(second_key, (), 0, SEQS)
    shortest = (longest + jax.random.randint(third_key, (), 1, SEQS)) % SEQS
    rows_index = jnp.arange(SEQS)
    drawn = jnp.where(rows_index == longest, CTX, drawn)
    drawn = jnp.where(rows_index == shortest, 1, drawn)
    return drawn.astype(jnp.int32)


def raised(entries, rng, source, target, shards_of, factor):
    def block_of(dim):
        return (jnp.arange(entries.shape[dim]) // (entries.shape[dim] // shards_of)).reshape((-1,) + (1,) * (entries.ndim - 1 - dim))

    near = jax.random.permutation(rng, shards_of)[block_of(target)]
    far = (block_of(target) + shards_of // 2) % shards_of
    return jnp.where((block_of(source) == near) | (block_of(source) == far), factor * entries, entries)


def levels(rng, dims, shards, smallest, largest):
    gain, own = 1.0, jax.random.fold_in(rng, 6)
    for dim, parts in shards:
        steps = jnp.exp(jax.random.uniform(jax.random.fold_in(own, dim), (parts,), jnp.float32, smallest / len(shards), largest / len(shards)))
        gain = gain * jnp.repeat(steps, dims[dim] // parts).reshape([-1 if axis == dim else 1 for axis in range(len(dims))])
    return gain


def scatter_about(own_key, dims, spread, limit, pieces=(), held_as=jnp.bfloat16):
    entries = spread * jax.random.normal(own_key, dims, jnp.float32)
    if pieces:
        entries = entries * levels(own_key, dims, pieces, -0.22, 0.18)
    return jnp.clip(entries, -limit, limit).astype(held_as)


def heavy_noise(rng, extent, deviation, limit, cuts, heavy, held_as=jnp.bfloat16):
    values = deviation * jax.random.normal(rng, extent, jnp.float32)
    if cuts:
        values = values * levels(rng, extent, cuts, -0.22, 0.18)
    return jnp.clip(raised(values, jax.random.fold_in(rng, 3), *heavy), -limit, limit).astype(held_as)


def setup_inputs(seed: int = 0) -> dict:
    arg_keys = jax.random.split(jax.random.key(seed), 13)
    return {
        "hidden_in": scatter_about(arg_keys[0], (SEQS, D), 1.0, 6.0, ((0, 32), (1, 4))),
        "query": draw_query(jax.random.fold_in(arg_keys[12], 71), 0),
        "new_key": scatter_about(arg_keys[2], (SEQS, KVH * HD), 2.0, 8.0, ((0, 32), (1, 4))),
        "new_value": scatter_about(arg_keys[3], (SEQS, KVH * HD), 1.0, 6.0, ((0, 32), (1, 4))),
        "cache_keys": draw_cache_keys(jax.random.fold_in(arg_keys[12], 71), 0),
        "cache_values": scatter_about(arg_keys[5], (SEQS, CTX, KVH * HD), 1.0, 6.0, ((1, 32), (2, 4))),
        "lengths": draw_lengths(jax.random.fold_in(arg_keys[12], 71), 0),
        "out_weight": scatter_about(arg_keys[7], (H * HD, D), (H * HD) ** -0.5, 0.09375, ((0, 4), (1, 32))),
        "norm_gain": jnp.clip(1.0 + 0.18 * jax.random.normal(arg_keys[8], (D,), jnp.float32), 0.1, 1.9),
        "w_gate": scatter_about(arg_keys[9], (D, FF), D ** -0.5, 0.09375, ((1, 128),)),
        "w_up": scatter_about(arg_keys[10], (D, FF), D ** -0.5, 0.09375, ((1, 128),)),
        "w_down": heavy_noise(arg_keys[11], (FF, D), FF ** -0.5, 0.1875, ((0, 128),), (0, 1, 128, 5.5)),
    }


EPSILON = 1e-05
MASKED = -1e+30

def attend_one(seq_items):
    query_row, key_row, value_row, cache_k, cache_v, length = seq_items
    group_size = H // KVH
    factor = 1.0 / math.sqrt(HD)
    queries = query_row.astype(jnp.float32).reshape(KVH, group_size, HD)
    keys_view = cache_k.astype(jnp.float32).reshape(N_CTX, CTX_DEV, KVH, HD)
    values_view = cache_v.astype(jnp.float32).reshape(N_CTX, CTX_DEV, KVH, HD)
    scores = jnp.einsum('kgd,jtkd->jkgt', queries, keys_view) * factor
    places = jnp.arange(N_CTX * CTX_DEV, dtype=jnp.int32).reshape(N_CTX, 1, 1, CTX_DEV)
    is_valid = places < length
    block_max = lax.optimization_barrier(jnp.max(jnp.where(is_valid, scores, MASKED), axis=-1))
    weights = jnp.where(is_valid, jnp.exp(scores - block_max[..., None]), 0.0).astype(jnp.bfloat16)
    block_den = lax.optimization_barrier(jnp.sum(weights.astype(jnp.float32), axis=-1))
    block_num = jnp.einsum('jkgt,jtkd->jkgd', weights.astype(jnp.float32), values_view)
    peak_score = lax.optimization_barrier(jnp.max(block_max, axis=0))
    rescale = jnp.exp(block_max - peak_score)
    cache_den = lax.optimization_barrier(jnp.sum(block_den * rescale, axis=0))
    cache_num = lax.optimization_barrier(jnp.sum(block_num * rescale[..., None], axis=0))
    own_score = jnp.einsum('kgd,kd->kg', queries, key_row.astype(jnp.float32).reshape(KVH, HD)) * factor
    top_score = jnp.maximum(peak_score, own_score)
    keep_share = jnp.exp(peak_score - top_score)
    fresh_share = jnp.exp(own_score - top_score)
    numerator = cache_num * keep_share[..., None] + fresh_share[..., None] * value_row.astype(jnp.float32).reshape(KVH, 1, HD)
    return (numerator / (cache_den * keep_share + fresh_share)[..., None]).reshape(H * HD).astype(jnp.bfloat16)

def reference(hidden_in, query, new_key, new_value, cache_keys, cache_values, lengths, out_weight, norm_gain, w_gate, w_up, w_down):
    attention = lax.map(attend_one, (query, new_key, new_value, cache_keys, cache_values, lengths))
    mid_stream = hidden_in.astype(jnp.float32) + jnp.dot(attention, out_weight, preferred_element_type=jnp.float32)
    mean_square = lax.optimization_barrier(jnp.sum(mid_stream * mid_stream, axis=1)) / D
    normed = (mid_stream * lax.rsqrt(mean_square + EPSILON)[:, None] * norm_gain).astype(jnp.bfloat16)
    gate_out = jnp.dot(normed, w_gate, preferred_element_type=jnp.float32)
    up_out = jnp.dot(normed, w_up, preferred_element_type=jnp.float32)
    activation = (jax.nn.silu(gate_out) * up_out).astype(jnp.bfloat16)
    return (mid_stream + jnp.dot(activation, w_down, preferred_element_type=jnp.float32)).astype(jnp.bfloat16)
```

```python
import math

import jax
import jax.numpy as jnp
from jax import lax
from jax.experimental import pallas as pl
from jax.experimental.pallas import tpu as pltpu
from jax.sharding import Mesh
from jax.sharding import PartitionSpec as P

D = 4096
HD = 128
EPSILON = 1e-05
MASKED = -1e30
F32 = jnp.float32
BF16 = jnp.bfloat16

CHIPS = 16
TP = 4
SEQS = 32
HALF = 16
HEADS = 8
STEP = 4
ROWS = HEADS * HALF
MSG = ROWS + 16

VMEM_LIMIT = 48 * 1024 * 1024


def pack_lse(lse_of_head):
    lane = lax.broadcasted_iota(jnp.int32, (HALF, 128), 1)
    packed = jnp.zeros((HALF, 128), F32)
    for h in range(HEADS):
        value = lse_of_head(h)
        high = value.astype(BF16).astype(F32)
        rest = value - high
        middle = rest.astype(BF16).astype(F32)
        low = rest - middle
        packed = jnp.where(lane == h, high, packed)
        packed = jnp.where(lane == HEADS + h, middle, packed)
        packed = jnp.where(lane == 2 * HEADS + h, low, packed)
    return packed.astype(BF16)


def attend_kernel(
    lengths, gathered, keys, values, own_key, own_value, sent, kept, kept_lse, hidden_part, outs, lses, rows
):
    step = pl.program_id(0)
    chip, core, plane = lax.axis_index("p"), lax.axis_index("k"), lax.axis_index("t")
    ctx_dev = keys.shape[1]
    factor = 1.0 / math.sqrt(HD)
    first = (chip * 2 + core) * ctx_dev
    head = lax.broadcasted_iota(jnp.int32, (HEADS, HD), 0)
    zero = jnp.zeros((HEADS, HD), BF16)
    for i in range(STEP):
        b = step * STEP + i
        j = step * (STEP // 2) + i // 2
        query = gathered[b][:HEADS]
        wide = jnp.concatenate(
            [jnp.where(head < HEADS // 2, query, zero), jnp.where(head >= HEADS // 2, query, zero)], axis=1
        )
        scores = (
            lax.dot_general(wide, keys[i], (((1,), (1,)), ((), ())), preferred_element_type=F32) * factor
        )
        place = first + lax.broadcasted_iota(jnp.int32, scores.shape, 1)
        valid = place < lengths[b]
        top = jnp.max(jnp.where(valid, scores, MASKED), axis=1, keepdims=True)
        weights = jnp.where(valid, jnp.exp(scores - top), 0.0).astype(BF16)
        den = jnp.sum(weights.astype(F32), axis=1, keepdims=True)
        num = jnp.dot(weights, values[i], preferred_element_type=F32)
        num = jnp.where(head < HEADS // 2, num[:, :HD], num[:, HD:])
        some = den > 0.0
        safe = jnp.where(some, den, 1.0)
        lse = jnp.where(some, top + jnp.log(safe), MASKED)
        outs[i % 2, pl.ds(j, HEADS, stride=HALF), :] = num / safe
        lses[i % 2, pl.ds(j, HEADS, stride=HALF), :] = jnp.broadcast_to(lse, (HEADS, HD))

    @pl.when(step == pl.num_programs(0) - 1)
    def _():
        query = gathered[chip * 2 + core][:HEADS].astype(F32)
        key, value = own_key[...].astype(F32), own_value[...].astype(F32)
        key = jnp.where(head < HEADS // 2, key[:, :HD], key[:, HD:])
        value = jnp.where(head < HEADS // 2, value[:, :HD], value[:, HD:])
        own = jnp.sum(query * key, axis=1, keepdims=True) * factor
        place = pl.ds(chip, HEADS, stride=HALF)
        block, block_lse = outs[core, place, :], lses[core, place, :]
        top = jnp.maximum(block_lse, own)
        keep, fresh = jnp.exp(block_lse - top), jnp.exp(own - top)
        total = keep + fresh
        outs[core, place, :] = (block * keep + value * fresh) / total
        lses[core, place, :] = top + jnp.log(total)
        kept[...] = outs[core]
        kept_lse[...] = lses[core]
        other = 1 - core
        sent[:ROWS, :] = outs[other].astype(BF16)
        sent[ROWS:, :] = pack_lse(lambda h: lses[other, h * HALF : (h + 1) * HALF, :])
        rows[...] = gathered[...].reshape(SEQS * 16, HD).astype(F32)
        column = core * 16 + HEADS + (chip % 4) * 2
        mine = plane == chip // 4
        for i in range(2):
            part = rows[pl.ds(column + i, HALF, stride=32), :]
            hidden_part[i] = jnp.where(mine, part, 0.0)


def merge_kernel(kept, kept_lse, came, message):
    packed = came[ROWS:, :].astype(F32)
    merged_lse = []
    for h in range(HEADS):
        place = slice(h * HALF, (h + 1) * HALF)
        mine = kept_lse[place, :]
        theirs = (packed[:, h : h + 1] + packed[:, HEADS + h : HEADS + h + 1]) + packed[
            :, 2 * HEADS + h : 2 * HEADS + h + 1
        ]
        top = jnp.maximum(mine, theirs)
        left, right = jnp.exp(mine - top), jnp.exp(theirs - top)
        total = left + right
        block = (kept[place, :] * left + came[place, :].astype(F32) * right) / total
        message[:, place, :] = jnp.broadcast_to(block.astype(BF16)[None], (CHIPS, HALF, HD))
        merged_lse.append(top + jnp.log(total))
    packed = pack_lse(lambda h: merged_lse[h])
    message[:, ROWS:, :] = jnp.broadcast_to(packed[None], (CHIPS, 16, HD))


def project_kernel(blocks, weight, other_weight, hidden_part, message):
    core = lax.axis_index("k")
    lse = []
    for s in range(CHIPS):
        packed = blocks[s, ROWS:, :].astype(F32)
        lse.append((packed + pltpu.roll(packed, 128 - HEADS, 1)) + pltpu.roll(packed, 128 - 2 * HEADS, 1))
    top = lse[0]
    for s in range(1, CHIPS):
        top = jnp.maximum(top, lse[s])
    share = [jnp.exp(x - top) for x in lse]
    total = share[0]
    for s in range(1, CHIPS):
        total = total + share[s]
    share = [x / total for x in share]
    columns = []
    for h in range(HEADS):
        place = slice(h * HALF, (h + 1) * HALF)
        acc = jnp.zeros((HALF, HD), F32)
        for s in range(CHIPS):
            acc = acc + share[s][:, h : h + 1] * blocks[s, place, :].astype(F32)
        columns.append(acc.astype(BF16))
    attention = jnp.concatenate(columns, axis=1)
    mine = jnp.dot(attention, weight[...], preferred_element_type=F32)
    other = jnp.dot(attention, other_weight[...], preferred_element_type=F32)
    low = jnp.where(core == 0, mine, other) + hidden_part[0]
    high = jnp.where(core == 0, other, mine) + hidden_part[1]
    message[:, :HALF, :] = jnp.broadcast_to(low.astype(BF16)[None], message[:, :HALF, :].shape)
    message[:, HALF:, :] = jnp.broadcast_to(high.astype(BF16)[None], message[:, :HALF, :].shape)


def feed_kernel(
    parts, gain0, gain1, gain2, gain3, gate0, gate1, up0, up1, down0, down1, message, mid_row, mid, gains
):
    chip, plane = lax.axis_index("p"), lax.axis_index("t")
    for i, gain in enumerate((gain0, gain1, gain2, gain3)):
        at = lax.rem(plane + i, TP) * 8
        gains[pl.ds(pl.multiple_of(at, 8), 8), :] = gain[...]
    square = jnp.zeros((HALF, HD), F32)
    for c in range(2 * CHIPS):
        place = slice((c % 2) * HALF, (c % 2 + 1) * HALF)
        piece = parts[(c // 2) * TP, place, :].astype(F32)
        for t in range(1, TP):
            piece = piece + parts[(c // 2) * TP + t, place, :].astype(F32)
        mid[c * HALF : (c + 1) * HALF, :] = piece
        square = square + piece * piece
    scale = lax.rsqrt(jnp.sum(square, axis=1, keepdims=True) / D + EPSILON)
    mid_row[...] = mid[pl.ds(plane * 8 * HALF + chip, 8, stride=HALF), :]
    normed = jnp.concatenate(
        [
            (mid[c * HALF : (c + 1) * HALF, :] * scale * gains[c : c + 1, :]).astype(BF16)
            for c in range(2 * CHIPS)
        ],
        axis=1,
    )

    def hidden_units(gate, up):
        gate_out = jnp.dot(normed, gate[...], preferred_element_type=F32)
        up_out = jnp.dot(normed, up[...], preferred_element_type=F32)
        return (gate_out / (1.0 + jnp.exp(-gate_out)) * up_out).astype(BF16)

    act0, act1 = hidden_units(gate0, up0), hidden_units(gate1, up1)
    wide = 512
    for n in range(D // wide):
        place = slice(n * wide, (n + 1) * wide)
        partial = jnp.dot(act0, down0[:, place], preferred_element_type=F32) + jnp.dot(
            act1, down1[:, place], preferred_element_type=F32
        )
        for i in range(wide // HD):
            c = n * (wide // HD) + i
            message[pl.ds(c, HALF, stride=2 * CHIPS), :] = partial[:, i * HD : (i + 1) * HD]


def sum_kernel(parts, mid_row, out):
    total = parts[0]
    for s in range(1, CHIPS * TP):
        total = total + parts[s]
    total = (mid_row[...] + total).astype(BF16)
    for r in range(8):
        out[:, r * HD : (r + 1) * HD] = total[r : r + 1, :]


def vmem():
    return pl.BlockSpec(memory_space=pltpu.VMEM)


def call(kernel, out_shape, operands, scratch=()):
    return pl.pallas_call(
        kernel,
        out_shape=out_shape,
        in_specs=[vmem()] * len(operands),
        out_specs=jax.tree.map(lambda _: vmem(), out_shape),
        scratch_shapes=list(scratch),
        compiler_params=pltpu.CompilerParams(vmem_limit_bytes=VMEM_LIMIT),
    )(*operands)


def shards(
    hidden_in,
    query,
    new_key,
    new_value,
    cache_keys,
    cache_values,
    lengths,
    out_weight,
    norm_gain,
    w_gate,
    w_up,
    w_down,
):
    def other_core(x):
        return lax.ppermute(x, "k", [(0, 1), (1, 0)])

    gain = norm_gain.reshape(8, HD)
    gains = [gain] + [lax.ppermute(gain, "t", [((i + n) % TP, i) for i in range(TP)]) for n in range(1, TP)]
    other_out_weight, other_gate, other_up, other_down = map(other_core, (out_weight, w_gate, w_up, w_down))

    own = jnp.concatenate([query.reshape(HEADS, HD), hidden_in.reshape(8, HD)], axis=0)
    gathered = lax.all_to_all(jnp.broadcast_to(own[None], (SEQS, 16, HD)), ("p", "k"), 0, 0, tiled=True)

    ctx_dev, width = cache_keys.shape[1], cache_keys.shape[2]
    sent, kept, kept_lse, hidden_part = pl.pallas_call(
        attend_kernel,
        out_shape=(
            jax.ShapeDtypeStruct((MSG, HD), BF16),
            jax.ShapeDtypeStruct((ROWS, HD), F32),
            jax.ShapeDtypeStruct((ROWS, HD), F32),
            jax.ShapeDtypeStruct((2, HALF, HD), F32),
        ),
        grid=(SEQS // STEP,),
        in_specs=[
            pl.BlockSpec(memory_space=pltpu.SMEM),
            vmem(),
            pl.BlockSpec((STEP, ctx_dev, width), lambda g: (g, 0, 0)),
            pl.BlockSpec((STEP, ctx_dev, width), lambda g: (g, 0, 0)),
            vmem(),
            vmem(),
        ],
        out_specs=(vmem(), vmem(), vmem(), vmem()),
        scratch_shapes=[
            pltpu.VMEM((2, ROWS, HD), F32),
            pltpu.VMEM((2, ROWS, HD), F32),
            pltpu.VMEM((SEQS * 16, HD), F32),
        ],
        compiler_params=pltpu.CompilerParams(vmem_limit_bytes=VMEM_LIMIT),
    )(lengths, gathered, cache_keys, cache_values, new_key, new_value)

    came = other_core(sent)
    blocks = call(merge_kernel, jax.ShapeDtypeStruct((CHIPS, MSG, HD), BF16), (kept, kept_lse, came))
    blocks = lax.all_to_all(blocks, "p", 0, 0, tiled=True)
    columns = call(
        project_kernel,
        jax.ShapeDtypeStruct((CHIPS * TP, 2 * HALF, HD), BF16),
        (blocks, out_weight, other_out_weight, hidden_part),
    )
    columns = lax.all_to_all(columns, ("p", "t"), 0, 0, tiled=True)
    partial, mid_row = call(
        feed_kernel,
        (jax.ShapeDtypeStruct((CHIPS * TP * 8, HD), F32), jax.ShapeDtypeStruct((8, HD), F32)),
        (columns, *gains, w_gate, other_gate, w_up, other_up, w_down, other_down),
        (pltpu.VMEM((2 * CHIPS * HALF, HD), F32), pltpu.VMEM((2 * CHIPS, HD), F32)),
    )
    partial = lax.all_to_all(partial.reshape(CHIPS * TP, 8, HD), ("p", "t"), 0, 0, tiled=True)
    return call(sum_kernel, jax.ShapeDtypeStruct((1, 8 * HD), BF16), (partial, mid_row))


def solution(mesh):
    cut = Mesh(mesh.devices.reshape(CHIPS, 2, TP), ("p", "k", "t"))
    ctx, tp = ("p", "k"), "t"
    return jax.shard_map(
        shards,
        mesh=cut,
        in_specs=(
            P(ctx, tp),
            P(ctx, tp),
            P(ctx, tp),
            P(ctx, tp),
            P(None, ctx, tp),
            P(None, ctx, tp),
            P(),
            P(tp, ctx),
            P(tp),
            P(None, ("p", "k", "t")),
            P(None, ("p", "k", "t")),
            P(("p", "k", "t"), None),
        ),
        out_specs=P(ctx, tp),
        check_vma=False,
    )
```

```python
import functools
import math

import jax
import jax.numpy as jnp
from jax import lax
from jax.experimental import pallas as pl
from jax.experimental.pallas import tpu as pltpu
from jax.sharding import Mesh
from jax.sharding import PartitionSpec as P

D = 4096
HD = 128
EPSILON = 1e-05
MASKED = -1e30
F32 = jnp.float32
BF16 = jnp.bfloat16

CHIPS = 16
TP = 4
SEQS = 32
HALF = 16
HEADS = 8
GROUPS = (6, 8, 8, 6, 4)
ROWS = HEADS * HALF
MSG = ROWS + 16

SMALL = 8 * 1024 * 1024
LARGE = 24 * 1024 * 1024


def pack_lse(lse_of_head):
    lane = lax.broadcasted_iota(jnp.int32, (HALF, 128), 1)
    packed = jnp.zeros((HALF, 128), F32)
    for h in range(HEADS):
        for i, part in enumerate(addends(lse_of_head(h))):
            packed = jnp.where(lane == i * HEADS + h, part, packed)
    return packed.astype(BF16)


def addends(x):
    high = x.astype(BF16).astype(F32)
    middle = (x - high).astype(BF16).astype(F32)
    return high, middle, x - high - middle


def copy_in(sources, targets, arrived):
    copies = [pltpu.make_async_copy(a, b, arrived.at[i]) for i, (a, b) in enumerate(zip(sources, targets))]
    for copy in copies:
        copy.start()
    return copies


def start_kernel(*refs):
    sources, (message, own, limits), landed, arrived = refs[:5], refs[5:8], refs[8:13], refs[13]
    for copy in copy_in(sources, landed, arrived):
        copy.wait()
    query, hidden, own_key, own_value, lengths = landed

    def rows(x):
        x = x[...].astype(F32)
        return jnp.concatenate([x[:, r * HD : (r + 1) * HD] for r in range(8)], axis=0)

    def heads(x):
        x = x[...].astype(F32)
        return jnp.concatenate([x[:, (h // 4) * HD : (h // 4 + 1) * HD] for h in range(HEADS)], axis=0)

    queries = rows(query)
    both = jnp.concatenate([queries, rows(hidden)], axis=0).astype(BF16)
    message[...] = jnp.broadcast_to(both[None], message.shape)
    score = jnp.sum(queries * heads(own_key), axis=1, keepdims=True) * (1.0 / math.sqrt(HD))
    own[0] = jnp.broadcast_to(score, (HEADS, HD))
    own[1] = heads(own_value)
    for b in range(SEQS):
        limits[b : b + 1, :] = jnp.full((1, HD), lengths[b], jnp.int32)


def first_kernel(keys, values, first_keys, first_values, arrived):
    count = first_keys.shape[0]
    for copy in copy_in((keys.at[:count], values.at[:count]), (first_keys, first_values), arrived):
        copy.wait()


def attend_kernel(
    limits,
    gathered,
    own,
    first_keys,
    first_values,
    cache_keys,
    cache_values,
    sent,
    kept,
    kept_lse,
    hidden_part,
    later_keys,
    later_values,
    outs,
    lses,
    rows,
    arrived,
):
    chip, core, plane = lax.axis_index("p"), lax.axis_index("k"), lax.axis_index("t")
    first, ctx_dev = first_keys.shape[:2]
    factor = 1.0 / math.sqrt(HD)
    copies, at = [()], first
    for n, group in enumerate(GROUPS[1:]):
        source, target = pl.ds(at, group), pl.ds(at - first, group)
        copies.append(
            copy_in(
                (cache_keys.at[source], cache_values.at[source]),
                (later_keys.at[target], later_values.at[target]),
                arrived.at[n],
            )
        )
        at += group

    def block(b, early, later):
        return early[b] if b < first else later[b - first]

    head = lax.broadcasted_iota(jnp.int32, (HEADS, HD), 0)
    zero = jnp.zeros((HEADS, HD), BF16)
    places = (chip * 2 + core) * ctx_dev + lax.broadcasted_iota(jnp.int32, (HEADS, ctx_dev), 1)

    def score(b):
        query = gathered[b][:HEADS]
        wide = jnp.concatenate(
            [jnp.where(head < HEADS // 2, query, zero), jnp.where(head >= HEADS // 2, query, zero)], axis=1
        )
        return lax.dot_general(wide, block(b, first_keys, later_keys), (((1,), (1,)), ((), ())), preferred_element_type=F32) * factor

    def soften(b, scores):
        limit = limits[b : b + 1, :]
        valid = places < jnp.concatenate([limit] * (ctx_dev // HD), axis=1)
        top = jnp.max(jnp.where(valid, scores, MASKED), axis=1, keepdims=True)
        weights = jnp.where(valid, jnp.exp(scores - top), 0.0).astype(BF16)
        return top, weights, jnp.sum(weights.astype(F32), axis=1, keepdims=True)

    def collect(b, top, weights, den):
        num = jnp.dot(weights, block(b, first_values, later_values), preferred_element_type=F32)
        num = jnp.where(head < HEADS // 2, num[:, :HD], num[:, HD:])
        some = den > 0.0
        safe = jnp.where(some, den, 1.0)
        return num / safe, jnp.where(some, top + jnp.log(safe), MASKED)

    at = 0
    for group, pair in zip(GROUPS, copies):
        for copy in pair:
            copy.wait()
        sequences = range(at, at + group)
        at += group
        scores = [score(b) for b in sequences]
        softened = [soften(b, x) for b, x in zip(sequences, scores)]
        collected = [collect(b, *x) for b, x in zip(sequences, softened)]
        for b, (out, lse) in zip(sequences, collected):
            outs[b % 2, pl.ds(b // 2, HEADS, stride=HALF), :] = out
            lses[b % 2, pl.ds(b // 2, HEADS, stride=HALF), :] = jnp.broadcast_to(lse, (HEADS, HD))

    fresh_score, value = own[0], own[1]
    place = pl.ds(chip, HEADS, stride=HALF)
    cached, block_lse = outs[core, place, :], lses[core, place, :]
    top = jnp.maximum(block_lse, fresh_score)
    keep, fresh = jnp.exp(block_lse - top), jnp.exp(fresh_score - top)
    total = keep + fresh
    outs[core, place, :] = (cached * keep + value * fresh) / total
    lses[core, place, :] = top + jnp.log(total)
    kept[...] = outs[core]
    kept_lse[...] = lses[core]
    other = 1 - core
    sent[:ROWS, :] = outs[other].astype(BF16)
    sent[ROWS:, :] = pack_lse(lambda h: lses[other, h * HALF : (h + 1) * HALF, :])
    rows[...] = gathered[...].reshape(SEQS * 16, HD).astype(F32)
    column = core * 16 + HEADS + (chip % 4) * 2
    for i in range(2):
        part = rows[pl.ds(column + i, HALF, stride=32), :]
        hidden_part[i] = jnp.where(plane == chip // 4, part, 0.0)


def merge_kernel(kept, kept_lse, came, gain, message, gain_out):
    gain_out[...] = gain[...]
    packed = came[ROWS:, :].astype(F32)
    merged_lse = []
    for h in range(HEADS):
        place = slice(h * HALF, (h + 1) * HALF)
        mine = kept_lse[place, :]
        theirs = (packed[:, h : h + 1] + packed[:, HEADS + h : HEADS + h + 1]) + packed[
            :, 2 * HEADS + h : 2 * HEADS + h + 1
        ]
        top = jnp.maximum(mine, theirs)
        left, right = jnp.exp(mine - top), jnp.exp(theirs - top)
        total = left + right
        block = (kept[place, :] * left + came[place, :].astype(F32) * right) / total
        message[:, place, :] = jnp.broadcast_to(block.astype(BF16)[None], (CHIPS, HALF, HD))
        merged_lse.append(top + jnp.log(total))
    packed = pack_lse(lambda h: merged_lse[h])
    message[:, ROWS:, :] = jnp.broadcast_to(packed[None], (CHIPS, 16, HD))


def project_kernel(blocks, hidden_part, gain0, gain1, gain2, gain3, *refs):
    sources, message, gains, landed, arrived = refs[:8], refs[8], refs[9], refs[10:18], refs[18]
    copies = copy_in(sources, landed, arrived)
    weight, other_weight = landed[6:]
    core, plane = lax.axis_index("k"), lax.axis_index("t")
    for i, gain in enumerate((gain0, gain1, gain2, gain3)):
        at = pl.multiple_of(lax.rem(plane + i, TP) * 8, 8)
        gains[pl.ds(at, 8), :] = gain[...]
    lse = []
    for s in range(CHIPS):
        packed = blocks[s, ROWS:, :].astype(F32)
        lse.append((packed + pltpu.roll(packed, 128 - HEADS, 1)) + pltpu.roll(packed, 128 - 2 * HEADS, 1))
    top = lse[0]
    for s in range(1, CHIPS):
        top = jnp.maximum(top, lse[s])
    share = [jnp.exp(x - top) for x in lse]
    total = share[0]
    for s in range(1, CHIPS):
        total = total + share[s]
    share = [x / total for x in share]
    columns = []
    for h in range(HEADS):
        place = slice(h * HALF, (h + 1) * HALF)
        acc = jnp.zeros((HALF, HD), F32)
        for s in range(CHIPS):
            acc = acc + share[s][:, h : h + 1] * blocks[s, place, :].astype(F32)
        columns.append(acc.astype(BF16))
    attention = jnp.concatenate(columns, axis=1)
    for copy in copies:
        copy.wait()
    mine = jnp.dot(attention, weight[...], preferred_element_type=F32)
    other = jnp.dot(attention, other_weight[...], preferred_element_type=F32)
    low, high = jnp.where(core == 0, mine, other), jnp.where(core == 0, other, mine)
    for i, rows in enumerate((low, high)):
        rows = (rows + hidden_part[i]).astype(BF16)
        message[:, i * HALF : (i + 1) * HALF, :] = jnp.broadcast_to(rows[None], (CHIPS * TP, HALF, HD))


def feed_kernel(parts, gains, gate0, up0, gate1, up1, down0, down1, message, mid_row, mid):
    chip, plane = lax.axis_index("p"), lax.axis_index("t")
    square = jnp.zeros((HALF, HD), F32)
    for c in range(2 * CHIPS):
        place = slice((c % 2) * HALF, (c % 2 + 1) * HALF)
        piece = parts[(c // 2) * TP, place, :].astype(F32)
        for t in range(1, TP):
            piece = piece + parts[(c // 2) * TP + t, place, :].astype(F32)
        mid[c * HALF : (c + 1) * HALF, :] = piece
        square = square + piece * piece
    scale = lax.rsqrt(jnp.sum(square, axis=1, keepdims=True) / D + EPSILON)
    mid_row[...] = mid[pl.ds(plane * 8 * HALF + chip, 8, stride=HALF), :]

    def normed_columns(c):
        return (mid[c * HALF : (c + 1) * HALF, :] * scale * gains[c : c + 1, :]).astype(BF16)

    normed = jnp.concatenate([normed_columns(c) for c in range(2 * CHIPS)], axis=1)

    def hidden_units(gate, up):
        over = (((1,), (1,)), ((), ()))
        gate_out = lax.dot_general(normed, gate[...], over, preferred_element_type=F32)
        up_out = lax.dot_general(normed, up[...], over, preferred_element_type=F32)
        return (gate_out / (1.0 + jnp.exp(-gate_out)) * up_out).astype(BF16)

    act0, act1 = hidden_units(gate0, up0), hidden_units(gate1, up1)
    wide = 512
    for n in range(D // wide):
        place = slice(n * wide, (n + 1) * wide)
        partial = jnp.dot(act0, down0[:, place], preferred_element_type=F32) + jnp.dot(
            act1, down1[:, place], preferred_element_type=F32
        )
        for i in range(wide // HD):
            c = n * (wide // HD) + i
            message[pl.ds(c, HALF, stride=2 * CHIPS), :] = partial[:, i * HD : (i + 1) * HD]


def sum_kernel(parts, mid_row, out):
    total = parts[0]
    for s in range(1, CHIPS * TP):
        total = total + parts[s]
    total = (mid_row[...] + total).astype(BF16)
    for r in range(8):
        out[:, r * HD : (r + 1) * HD] = total[r : r + 1, :]


def in_vmem(shape, dtype):
    return pltpu.VMEM(shape, dtype)


def stay(x):
    return pltpu.with_memory_space_constraint(x, pltpu.HBM)


def call(kernel, out_shape, operands, scratch=(), far=(), pinned=(), limit=SMALL, cost=None):
    vmem = pl.BlockSpec(memory_space=pltpu.VMEM)
    specs = [pl.BlockSpec(memory_space=pl.ANY) if i in far else vmem for i in range(len(operands))]
    return pl.pallas_call(
        kernel,
        out_shape=out_shape,
        in_specs=specs,
        out_specs=jax.tree.map(lambda _: vmem, out_shape, is_leaf=lambda x: not isinstance(x, tuple)),
        scratch_shapes=list(scratch),
        compiler_params=pltpu.CompilerParams(vmem_limit_bytes=limit),
        cost_estimate=cost,
    )(*(stay(x) if i in pinned else x for i, x in enumerate(operands)))


def shards(
    hidden_in,
    query,
    new_key,
    new_value,
    cache_keys,
    cache_values,
    lengths,
    out_weight,
    norm_gain,
    w_gate,
    w_up,
    w_down,
):
    def other_core(x):
        return lax.ppermute(x, "k", [(0, 1), (1, 0)])

    w_gate, w_up = w_gate.T, w_up.T
    other_out_weight, other_gate, other_up, other_down = map(other_core, (out_weight, w_gate, w_up, w_down))

    inputs = (query, hidden_in, new_key, new_value, lengths)
    message, own, limits = call(
        start_kernel,
        (in_vmem((SEQS, 16, HD), BF16), in_vmem((2, HEADS, HD), F32), in_vmem((SEQS, HD), jnp.int32)),
        inputs,
        [
            *(pltpu.VMEM(x.shape, x.dtype) for x in inputs[:4]),
            pltpu.SMEM(lengths.shape, jnp.int32),
            pltpu.SemaphoreType.DMA((5,)),
        ],
        far=range(5),
        pinned=range(5),
    )
    gathered = lax.all_to_all(message, ("p", "k"), 0, 0, tiled=True)
    first = (GROUPS[0], *cache_keys.shape[1:])
    later = (SEQS - GROUPS[0], *cache_keys.shape[1:])
    first_keys, first_values = call(
        first_kernel,
        (in_vmem(first, BF16), in_vmem(first, BF16)),
        (cache_keys, cache_values),
        [pltpu.SemaphoreType.DMA((2,))],
        far=range(2),
        pinned=range(2),
        cost=pl.CostEstimate(flops=0, bytes_accessed=4 * math.prod(first), transcendentals=0),
    )
    sent, kept, kept_lse, hidden_part = call(
        attend_kernel,
        (
            in_vmem((MSG, HD), BF16),
            in_vmem((ROWS, HD), F32),
            in_vmem((ROWS, HD), F32),
            in_vmem((2, HALF, HD), F32),
        ),
        (limits, gathered, own, first_keys, first_values, cache_keys, cache_values),
        [
            pltpu.VMEM(later, BF16),
            pltpu.VMEM(later, BF16),
            pltpu.VMEM((2, ROWS, HD), F32),
            pltpu.VMEM((2, ROWS, HD), F32),
            pltpu.VMEM((SEQS * 16, HD), F32),
            pltpu.SemaphoreType.DMA((len(GROUPS) - 1, 2)),
        ],
        far=(5, 6),
        pinned=(5, 6),
        limit=LARGE,
    )
    came = other_core(sent)
    blocks, gain = call(
        merge_kernel,
        (jax.ShapeDtypeStruct((CHIPS, MSG, HD), BF16), in_vmem((8, HD), F32)),
        (kept, kept_lse, came, norm_gain.reshape(8, HD)),
    )
    blocks = lax.all_to_all(blocks, "p", 0, 0, tiled=True)
    gains = [gain] + [lax.ppermute(gain, "t", [((i + n) % TP, i) for i in range(TP)]) for n in range(1, TP)]
    weights = (w_gate, w_up, other_gate, other_up, w_down, other_down)
    columns, gains, *weights = call(
        project_kernel,
        (
            in_vmem((CHIPS * TP, 2 * HALF, HD), BF16),
            in_vmem((TP * 8, HD), F32),
            *(in_vmem(w_down.shape, BF16) for _ in weights),
        ),
        (blocks, hidden_part, *gains, *weights, out_weight, other_out_weight),
        [*(pltpu.VMEM(out_weight.shape, BF16) for _ in range(2)), pltpu.SemaphoreType.DMA((8,))],
        far=range(6, 14),
        pinned=(6, 7, 10, 12),
    )
    columns = lax.all_to_all(columns, ("p", "t"), 0, 0, tiled=True)
    partial, mid_row = call(
        feed_kernel,
        (in_vmem((CHIPS * TP * 8, HD), F32), in_vmem((8, HD), F32)),
        (columns, gains, *weights),
        [pltpu.VMEM((2 * CHIPS * HALF, HD), F32)],
    )
    partial = lax.all_to_all(partial.reshape(CHIPS * TP, 8, HD), ("p", "t"), 0, 0, tiled=True)
    return call(sum_kernel, jax.ShapeDtypeStruct((1, 8 * HD), BF16), (partial, mid_row))


def solution(mesh):
    cut = Mesh(mesh.devices.reshape(CHIPS, 2, TP), ("p", "k", "t"))
    ctx, tp = ("p", "k"), "t"
    return jax.shard_map(
        shards,
        mesh=cut,
        in_specs=(
            P(ctx, tp),
            P(ctx, tp),
            P(ctx, tp),
            P(ctx, tp),
            P(None, ctx, tp),
            P(None, ctx, tp),
            P(),
            P(tp, ctx),
            P(tp),
            P(None, ("p", "k", "t")),
            P(None, ("p", "k", "t")),
            P(("p", "k", "t"), None),
        ),
        out_specs=P(ctx, tp),
        check_vma=False,
    )
```

```python
import functools
import math

import jax
import jax.numpy as jnp
from jax import lax
from jax.experimental import pallas as pl
from jax.experimental.pallas import tpu as pltpu
from jax.sharding import Mesh
from jax.sharding import PartitionSpec as P

D = 4096
HD = 128
EPSILON = 1e-05
MASKED = -1e30
F32 = jnp.float32
BF16 = jnp.bfloat16

CHIPS = 16
TP = 4
SEQS = 32
HALF = 16
HEADS = 8
GROUP = 8
ROWS = HEADS * HALF
MSG = ROWS + 16

SMALL = 8 * 1024 * 1024


def pack_lse(lse_of_head):
    lane = lax.broadcasted_iota(jnp.int32, (HALF, 128), 1)
    packed = jnp.zeros((HALF, 128), F32)
    for h in range(HEADS):
        for i, part in enumerate(addends(lse_of_head(h))):
            packed = jnp.where(lane == i * HEADS + h, part, packed)
    return packed.astype(BF16)


def addends(x):
    high = x.astype(BF16).astype(F32)
    middle = (x - high).astype(BF16).astype(F32)
    return high, middle, x - high - middle


def copy_in(sources, targets, arrived):
    copies = [pltpu.make_async_copy(a, b, arrived.at[i]) for i, (a, b) in enumerate(zip(sources, targets))]
    for copy in copies:
        copy.start()
    return copies


def start_kernel(*refs):
    sources, (message, own, limits), landed, arrived = refs[:5], refs[7:10], refs[10:15], refs[15]
    for copy in copy_in(sources, landed, arrived):
        copy.wait()
    query, hidden, own_key, own_value, lengths = landed

    def rows(x):
        x = x[...].astype(F32)
        return jnp.concatenate([x[:, r * HD : (r + 1) * HD] for r in range(8)], axis=0)

    def heads(x):
        x = x[...].astype(F32)
        return jnp.concatenate([x[:, (h // 4) * HD : (h // 4 + 1) * HD] for h in range(HEADS)], axis=0)

    queries = rows(query)
    both = jnp.concatenate([queries, rows(hidden)], axis=0).astype(BF16)
    message[...] = jnp.broadcast_to(both[None], message.shape)
    score = jnp.sum(queries * heads(own_key), axis=1, keepdims=True) * (1.0 / math.sqrt(HD))
    own[0] = jnp.broadcast_to(score, (HEADS, HD))
    own[1] = heads(own_value)
    for b in range(SEQS):
        limits[b : b + 1, :] = jnp.full((1, HD), lengths[b], jnp.int32)


def attend_kernel(limits, gathered, own, keys, values, sent, kept, kept_lse, hidden_part, outs, lses, rows):
    chip, core, plane = lax.axis_index("p"), lax.axis_index("k"), lax.axis_index("t")
    ctx_dev = keys.shape[1]
    factor = 1.0 / math.sqrt(HD)
    head = lax.broadcasted_iota(jnp.int32, (HEADS, HD), 0)
    zero = jnp.zeros((HEADS, HD), BF16)
    places = (chip * 2 + core) * ctx_dev + lax.broadcasted_iota(jnp.int32, (HEADS, ctx_dev), 1)

    def score(b):
        query = gathered[b][:HEADS]
        wide = jnp.concatenate(
            [jnp.where(head < HEADS // 2, query, zero), jnp.where(head >= HEADS // 2, query, zero)], axis=1
        )
        return lax.dot_general(wide, keys[b], (((1,), (1,)), ((), ())), preferred_element_type=F32) * factor

    def soften(b, scores):
        limit = limits[b : b + 1, :]
        valid = places < jnp.concatenate([limit] * (ctx_dev // HD), axis=1)
        top = jnp.max(jnp.where(valid, scores, MASKED), axis=1, keepdims=True)
        weights = jnp.where(valid, jnp.exp(scores - top), 0.0).astype(BF16)
        return top, weights, jnp.sum(weights.astype(F32), axis=1, keepdims=True)

    def collect(b, top, weights, den):
        num = jnp.dot(weights, values[b], preferred_element_type=F32)
        num = jnp.where(head < HEADS // 2, num[:, :HD], num[:, HD:])
        some = den > 0.0
        safe = jnp.where(some, den, 1.0)
        return num / safe, jnp.where(some, top + jnp.log(safe), MASKED)

    for at in range(0, SEQS, GROUP):
        sequences = range(at, at + GROUP)
        scores = [score(b) for b in sequences]
        softened = [soften(b, x) for b, x in zip(sequences, scores)]
        collected = [collect(b, *x) for b, x in zip(sequences, softened)]
        for b, (out, lse) in zip(sequences, collected):
            outs[b % 2, pl.ds(b // 2, HEADS, stride=HALF), :] = out
            lses[b % 2, pl.ds(b // 2, HEADS, stride=HALF), :] = jnp.broadcast_to(lse, (HEADS, HD))

    fresh_score, value = own[0], own[1]
    place = pl.ds(chip, HEADS, stride=HALF)
    cached, block_lse = outs[core, place, :], lses[core, place, :]
    top = jnp.maximum(block_lse, fresh_score)
    keep, fresh = jnp.exp(block_lse - top), jnp.exp(fresh_score - top)
    total = keep + fresh
    outs[core, place, :] = (cached * keep + value * fresh) / total
    lses[core, place, :] = top + jnp.log(total)
    kept[...] = outs[core]
    kept_lse[...] = lses[core]
    other = 1 - core
    sent[:ROWS, :] = outs[other].astype(BF16)
    sent[ROWS:, :] = pack_lse(lambda h: lses[other, h * HALF : (h + 1) * HALF, :])
    rows[...] = gathered[...].reshape(SEQS * 16, HD).astype(F32)
    column = core * 16 + HEADS + (chip % 4) * 2
    for i in range(2):
        part = rows[pl.ds(column + i, HALF, stride=32), :]
        hidden_part[i] = jnp.where(plane == chip // 4, part, 0.0)


def merge_kernel(kept, kept_lse, came, message):
    packed = came[ROWS:, :].astype(F32)
    merged_lse = []
    for h in range(HEADS):
        place = slice(h * HALF, (h + 1) * HALF)
        mine = kept_lse[place, :]
        theirs = (packed[:, h : h + 1] + packed[:, HEADS + h : HEADS + h + 1]) + packed[
            :, 2 * HEADS + h : 2 * HEADS + h + 1
        ]
        top = jnp.maximum(mine, theirs)
        left, right = jnp.exp(mine - top), jnp.exp(theirs - top)
        total = left + right
        block = (kept[place, :] * left + came[place, :].astype(F32) * right) / total
        message[:, place, :] = jnp.broadcast_to(block.astype(BF16)[None], (CHIPS, HALF, HD))
        merged_lse.append(top + jnp.log(total))
    packed = pack_lse(lambda h: merged_lse[h])
    message[:, ROWS:, :] = jnp.broadcast_to(packed[None], (CHIPS, 16, HD))


def project_kernel(blocks, hidden_part, gain, weight, other_weight, message):
    chip, core, plane = lax.axis_index("p"), lax.axis_index("k"), lax.axis_index("t")
    lse = []
    for s in range(CHIPS):
        packed = blocks[s, ROWS:, :].astype(F32)
        lse.append((packed + pltpu.roll(packed, 128 - HEADS, 1)) + pltpu.roll(packed, 128 - 2 * HEADS, 1))
    top = lse[0]
    for s in range(1, CHIPS):
        top = jnp.maximum(top, lse[s])
    share = [jnp.exp(x - top) for x in lse]
    total = share[0]
    for s in range(1, CHIPS):
        total = total + share[s]
    share = [x / total for x in share]
    columns = []
    for h in range(HEADS):
        place = slice(h * HALF, (h + 1) * HALF)
        acc = jnp.zeros((HALF, HD), F32)
        for s in range(CHIPS):
            acc = acc + share[s][:, h : h + 1] * blocks[s, place, :].astype(F32)
        columns.append(acc.astype(BF16))
    attention = jnp.concatenate(columns, axis=1)
    mine = jnp.dot(attention, weight[...], preferred_element_type=F32)
    other = jnp.dot(attention, other_weight[...], preferred_element_type=F32)
    low, high = jnp.where(core == 0, mine, other), jnp.where(core == 0, other, mine)
    for i, rows in enumerate((low, high)):
        rows = (rows + hidden_part[i]).astype(BF16)
        message[:, i * HALF : (i + 1) * HALF, :] = jnp.broadcast_to(rows[None], (CHIPS * TP, HALF, HD))
    rows = jnp.concatenate([*addends(gain[pl.ds((chip % 4) * 2, 2), :]), jnp.zeros((2, HD), F32)], axis=0)
    rows = jnp.where(plane == chip // 4, rows, 0.0).astype(BF16)
    message[:, 2 * HALF :, :] = jnp.broadcast_to(rows[None], (CHIPS * TP, 8, HD))


def feed_kernel(
    parts, gate0, up0, gate1, up1, down0, down1, message, mid_row, mid, sums, gains
):
    chip, plane = lax.axis_index("p"), lax.axis_index("t")
    for c in range(CHIPS):
        rows = parts[c * TP + c // 4, 2 * HALF :, :].astype(F32)
        gains[c * 8 : (c + 1) * 8, :] = (rows + pltpu.roll(rows, 6, 0)) + pltpu.roll(rows, 4, 0)
    square = jnp.zeros((HALF, HD), F32)
    for c in range(2 * CHIPS):
        place = slice((c % 2) * HALF, (c % 2 + 1) * HALF)
        piece = parts[(c // 2) * TP, place, :].astype(F32)
        for t in range(1, TP):
            piece = piece + parts[(c // 2) * TP + t, place, :].astype(F32)
        mid[c * HALF : (c + 1) * HALF, :] = piece
        square = square + piece * piece
    scale = lax.rsqrt(jnp.sum(square, axis=1, keepdims=True) / D + EPSILON)
    mid_row[...] = mid[pl.ds(plane * 8 * HALF + chip, 8, stride=HALF), :]

    def normed_columns(c):
        return (mid[c * HALF : (c + 1) * HALF, :] * scale * gains[c // 2 * 8 + c % 2 : c // 2 * 8 + c % 2 + 1, :]).astype(BF16)

    normed = jnp.concatenate([normed_columns(c) for c in range(2 * CHIPS)], axis=1)

    def hidden_units(gate, up):
        over = (((1,), (1,)), ((), ()))
        gate_out = lax.dot_general(normed, gate[...], over, preferred_element_type=F32)
        up_out = lax.dot_general(normed, up[...], over, preferred_element_type=F32)
        return (gate_out / (1.0 + jnp.exp(-gate_out)) * up_out).astype(BF16)

    act0, act1 = hidden_units(gate0, up0), hidden_units(gate1, up1)
    wide = 512
    for n in range(D // wide):
        place = slice(n * wide, (n + 1) * wide)
        partial = jnp.dot(act0, down0[:, place], preferred_element_type=F32) + jnp.dot(
            act1, down1[:, place], preferred_element_type=F32
        )
        for i in range(wide // HD):
            c = n * (wide // HD) + i
            sums[pl.ds(c, HALF, stride=2 * CHIPS), :] = partial[:, i * HD : (i + 1) * HD]
    message[...] = sums[...].astype(BF16)


def sum_kernel(parts, mid_row, out):
    total = parts[0].astype(F32)
    for s in range(1, CHIPS * TP):
        total = total + parts[s].astype(F32)
    total = (mid_row[...] + total).astype(BF16)
    for r in range(8):
        out[:, r * HD : (r + 1) * HD] = total[r : r + 1, :]


def in_vmem(shape, dtype):
    return pltpu.VMEM(shape, dtype)


def stay(x):
    return pltpu.with_memory_space_constraint(x, pltpu.HBM)


def held(x):
    return pltpu.with_memory_space_constraint(x, pltpu.VMEM)


def call(kernel, out_shape, operands, scratch=(), far=(), pinned=(), limit=SMALL, cost=None):
    vmem = pl.BlockSpec(memory_space=pltpu.VMEM)
    specs = [pl.BlockSpec(memory_space=pl.ANY) if i in far else vmem for i in range(len(operands))]
    return pl.pallas_call(
        kernel,
        out_shape=out_shape,
        in_specs=specs,
        out_specs=jax.tree.map(lambda _: vmem, out_shape, is_leaf=lambda x: not isinstance(x, tuple)),
        scratch_shapes=list(scratch),
        compiler_params=pltpu.CompilerParams(vmem_limit_bytes=limit),
        cost_estimate=cost,
    )(*(stay(x) if i in pinned else x for i, x in enumerate(operands)))


def shards(
    hidden_in,
    query,
    new_key,
    new_value,
    cache_keys,
    cache_values,
    lengths,
    out_weight,
    norm_gain,
    w_gate,
    w_up,
    w_down,
):
    def other_core(x):
        return lax.ppermute(x, "k", [(0, 1), (1, 0)])

    w_gate, w_up = w_gate.T, w_up.T
    inputs = (query, hidden_in, new_key, new_value, lengths)
    message, own, limits = call(
        start_kernel,
        (in_vmem((SEQS, 16, HD), BF16), in_vmem((2, HEADS, HD), F32), in_vmem((SEQS, HD), jnp.int32)),
        (*inputs, cache_keys, cache_values),
        [
            *(pltpu.VMEM(x.shape, x.dtype) for x in inputs[:4]),
            pltpu.SMEM(lengths.shape, jnp.int32),
            pltpu.SemaphoreType.DMA((5,)),
        ],
        far=range(7),
        pinned=range(7),
    )
    gathered = lax.all_to_all(message, ("p", "k"), 0, 0, tiled=True)
    *exchanged, gathered = lax.optimization_barrier((out_weight, w_gate, w_up, w_down, gathered))
    other_out_weight, other_gate, other_up, other_down = map(other_core, exchanged)
    sent, kept, kept_lse, hidden_part = call(
        attend_kernel,
        (
            in_vmem((MSG, HD), BF16),
            in_vmem((ROWS, HD), F32),
            in_vmem((ROWS, HD), F32),
            in_vmem((2, HALF, HD), F32),
        ),
        (limits, gathered, own, held(cache_keys), held(cache_values)),
        [
            pltpu.VMEM((2, ROWS, HD), F32),
            pltpu.VMEM((2, ROWS, HD), F32),
            pltpu.VMEM((SEQS * 16, HD), F32),
        ],
    )
    came = other_core(sent)
    blocks = call(merge_kernel, in_vmem((CHIPS, MSG, HD), BF16), (kept, kept_lse, came))
    blocks, other_gate, other_up, other_down, other_out_weight = lax.optimization_barrier(
        (blocks, other_gate, other_up, other_down, other_out_weight)
    )
    blocks = lax.all_to_all(blocks, "p", 0, 0, tiled=True)
    columns = call(
        project_kernel,
        in_vmem((CHIPS * TP, 2 * HALF + 8, HD), BF16),
        (blocks, hidden_part, norm_gain.reshape(8, HD), out_weight, other_out_weight),
    )
    columns = lax.all_to_all(columns, ("p", "t"), 0, 0, tiled=True)
    partial, mid_row = call(
        feed_kernel,
        (in_vmem((CHIPS * TP * 8, HD), BF16), in_vmem((8, HD), F32)),
        (columns, w_gate, w_up, other_gate, other_up, w_down, other_down),
        [
            pltpu.VMEM((2 * CHIPS * HALF, HD), F32),
            pltpu.VMEM((CHIPS * TP * 8, HD), F32),
            pltpu.VMEM((CHIPS * 8, HD), F32),
        ],
    )
    partial = lax.all_to_all(partial.reshape(CHIPS * TP, 8, HD), ("p", "t"), 0, 0, tiled=True)
    return call(sum_kernel, jax.ShapeDtypeStruct((1, 8 * HD), BF16), (partial, mid_row))


def solution(mesh):
    cut = Mesh(mesh.devices.reshape(CHIPS, 2, TP), ("p", "k", "t"))
    ctx, tp = ("p", "k"), "t"
    return jax.shard_map(
        shards,
        mesh=cut,
        in_specs=(
            P(ctx, tp),
            P(ctx, tp),
            P(ctx, tp),
            P(ctx, tp),
            P(None, ctx, tp),
            P(None, ctx, tp),
            P(),
            P(tp, ctx),
            P(tp),
            P(None, ("p", "k", "t")),
            P(None, ("p", "k", "t")),
            P(("p", "k", "t"), None),
        ),
        out_specs=P(ctx, tp),
        check_vma=False,
    )
```

```python
import functools
import math

import jax
import jax.numpy as jnp
from jax import lax
from jax.experimental import pallas as pl
from jax.experimental.pallas import tpu as pltpu
from jax.sharding import Mesh
from jax.sharding import PartitionSpec as P

D = 4096
HD = 128
EPSILON = 1e-05
MASKED = -1e30
F32 = jnp.float32
BF16 = jnp.bfloat16

CHIPS = 16
TP = 4
SEQS = 32
HALF = 16
HEADS = 8
GROUP = 8
ROWS = HEADS * HALF
MSG = ROWS + 8

SMALL = 8 * 1024 * 1024


def pack_lse(lse_of_head):
    lane = lax.broadcasted_iota(jnp.int32, (HALF, 128), 1)
    packed = jnp.zeros((HALF, 128), F32)
    for h in range(HEADS):
        for i, part in enumerate(addends(lse_of_head(h))):
            packed = jnp.where(lane == i * HEADS + h, part, packed)
    return (packed[:8] + pltpu.roll(packed[8:], 3 * HEADS, 1)).astype(BF16)


def unpack_lse(packed):
    packed = packed.astype(F32)
    packed = jnp.concatenate([packed, pltpu.roll(packed, 128 - 3 * HEADS, 1)], axis=0)
    return (packed + pltpu.roll(packed, 128 - HEADS, 1)) + pltpu.roll(packed, 128 - 2 * HEADS, 1)


def addends(x):
    high = x.astype(BF16).astype(F32)
    middle = (x - high).astype(BF16).astype(F32)
    return high, middle, x - high - middle


def copy_in(sources, targets, arrived):
    copies = [pltpu.make_async_copy(a, b, arrived.at[i]) for i, (a, b) in enumerate(zip(sources, targets))]
    for copy in copies:
        copy.start()
    return copies


def start_kernel(*refs):
    sources, (message, own, limits), landed, arrived = refs[:5], refs[7:10], refs[10:15], refs[15]
    for copy in copy_in(sources, landed, arrived):
        copy.wait()
    query, hidden, own_key, own_value, lengths = landed

    def rows(x):
        x = x[...].astype(F32)
        return jnp.concatenate([x[:, r * HD : (r + 1) * HD] for r in range(8)], axis=0)

    def heads(x):
        x = x[...].astype(F32)
        return jnp.concatenate([x[:, (h // 4) * HD : (h // 4 + 1) * HD] for h in range(HEADS)], axis=0)

    queries = rows(query)
    both = jnp.concatenate([queries, rows(hidden)], axis=0).astype(BF16)
    message[...] = jnp.broadcast_to(both[None], message.shape)
    score = jnp.sum(queries * heads(own_key), axis=1, keepdims=True) * (1.0 / math.sqrt(HD))
    own[0] = jnp.broadcast_to(score, (HEADS, HD))
    own[1] = heads(own_value)
    for b in range(SEQS):
        limits[b : b + 1, :] = jnp.full((1, HD), lengths[b], jnp.int32)


def attend(parity, limits, gathered, keys, values, outs, lses):
    chip, core = lax.axis_index("p"), lax.axis_index("k")
    ctx_dev = keys.shape[1]
    factor = 1.0 / math.sqrt(HD)
    head = lax.broadcasted_iota(jnp.int32, (HEADS, HD), 0)
    zero = jnp.zeros((HEADS, HD), BF16)
    places = (chip * 2 + core) * ctx_dev + lax.broadcasted_iota(jnp.int32, (HEADS, ctx_dev), 1)

    def score(b):
        query = gathered[b][:HEADS]
        wide = jnp.concatenate(
            [jnp.where(head < HEADS // 2, query, zero), jnp.where(head >= HEADS // 2, query, zero)], axis=1
        )
        return lax.dot_general(wide, keys[b], (((1,), (1,)), ((), ())), preferred_element_type=F32) * factor

    def soften(b, scores):
        limit = limits[pl.ds(b, 1), :]
        valid = places < jnp.concatenate([limit] * (ctx_dev // HD), axis=1)
        top = jnp.max(jnp.where(valid, scores, MASKED), axis=1, keepdims=True)
        weights = jnp.where(valid, jnp.exp(scores - top), 0.0).astype(BF16)
        return top, weights, jnp.sum(weights.astype(F32), axis=1, keepdims=True)

    def collect(b, top, weights, den):
        num = jnp.dot(weights, values[b], preferred_element_type=F32)
        num = jnp.where(head < HEADS // 2, num[:, :HD], num[:, HD:])
        some = den > 0.0
        safe = jnp.where(some, den, 1.0)
        return num / safe, jnp.where(some, top + jnp.log(safe), MASKED)

    for at in range(0, HALF, GROUP):
        sequences = [2 * j + parity for j in range(at, at + GROUP)]
        scores = [score(b) for b in sequences]
        softened = [soften(b, x) for b, x in zip(sequences, scores)]
        collected = [collect(b, *x) for b, x in zip(sequences, softened)]
        for i, (out, lse) in enumerate(collected):
            outs[pl.ds(at + i, HEADS, stride=HALF), :] = out
            lses[pl.ds(at + i, HEADS, stride=HALF), :] = jnp.broadcast_to(lse, (HEADS, HD))


def other_kernel(limits, gathered, keys, values, sent, outs, lses):
    attend(1 - lax.axis_index("k"), limits, gathered, keys, values, outs, lses)
    sent[:ROWS, :] = outs[...].astype(BF16)
    sent[ROWS:, :] = pack_lse(lambda h: lses[h * HALF : (h + 1) * HALF, :])


def kept_kernel(limits, gathered, own, keys, values, kept, kept_lse, hidden_part, rows):
    chip, core, plane = lax.axis_index("p"), lax.axis_index("k"), lax.axis_index("t")
    attend(core, limits, gathered, keys, values, kept, kept_lse)
    fresh_score, value = own[0], own[1]
    place = pl.ds(chip, HEADS, stride=HALF)
    cached, block_lse = kept[place, :], kept_lse[place, :]
    top = jnp.maximum(block_lse, fresh_score)
    keep, fresh = jnp.exp(block_lse - top), jnp.exp(fresh_score - top)
    total = keep + fresh
    kept[place, :] = (cached * keep + value * fresh) / total
    kept_lse[place, :] = top + jnp.log(total)
    rows[...] = gathered[...].reshape(SEQS * 16, HD).astype(F32)
    column = core * 16 + HEADS + (chip % 4) * 2
    for i in range(2):
        part = rows[pl.ds(column + i, HALF, stride=32), :]
        hidden_part[i] = jnp.where(plane == chip // 4, part, 0.0)


def merge_kernel(kept, kept_lse, came, message):
    came_lse = unpack_lse(came[ROWS:, :])
    merged_lse = []
    for h in range(HEADS):
        place = slice(h * HALF, (h + 1) * HALF)
        mine = kept_lse[place, :]
        theirs = came_lse[:, h : h + 1]
        top = jnp.maximum(mine, theirs)
        left, right = jnp.exp(mine - top), jnp.exp(theirs - top)
        total = left + right
        block = (kept[place, :] * left + came[place, :].astype(F32) * right) / total
        message[:, place, :] = jnp.broadcast_to(block.astype(BF16)[None], (CHIPS, HALF, HD))
        merged_lse.append(top + jnp.log(total))
    packed = pack_lse(lambda h: merged_lse[h])
    message[:, ROWS:, :] = jnp.broadcast_to(packed[None], (CHIPS, 8, HD))


def project_kernel(blocks, hidden_part, gain, weight, other_weight, message):
    chip, core, plane = lax.axis_index("p"), lax.axis_index("k"), lax.axis_index("t")
    lse = []
    for s in range(CHIPS):
        lse.append(unpack_lse(blocks[s, ROWS:, :]))
    top = lse[0]
    for s in range(1, CHIPS):
        top = jnp.maximum(top, lse[s])
    share = [jnp.exp(x - top) for x in lse]
    total = share[0]
    for s in range(1, CHIPS):
        total = total + share[s]
    share = [x / total for x in share]
    columns = []
    for h in range(HEADS):
        place = slice(h * HALF, (h + 1) * HALF)
        acc = jnp.zeros((HALF, HD), F32)
        for s in range(CHIPS):
            acc = acc + share[s][:, h : h + 1] * blocks[s, place, :].astype(F32)
        columns.append(acc.astype(BF16))
    attention = jnp.concatenate(columns, axis=1)
    mine = jnp.dot(attention, weight[...], preferred_element_type=F32)
    other = jnp.dot(attention, other_weight[...], preferred_element_type=F32)
    low, high = jnp.where(core == 0, mine, other), jnp.where(core == 0, other, mine)
    for i, rows in enumerate((low, high)):
        rows = (rows + hidden_part[i]).astype(BF16)
        message[:, i * HALF : (i + 1) * HALF, :] = jnp.broadcast_to(rows[None], (CHIPS * TP, HALF, HD))
    rows = jnp.concatenate([*addends(gain[pl.ds((chip % 4) * 2, 2), :]), jnp.zeros((2, HD), F32)], axis=0)
    rows = jnp.where(plane == chip // 4, rows, 0.0).astype(BF16)
    message[:, 2 * HALF :, :] = jnp.broadcast_to(rows[None], (CHIPS * TP, 8, HD))


def feed_kernel(
    parts, gate0, up0, gate1, up1, down0, down1, message, mid_row, mid, sums, gains
):
    chip, plane = lax.axis_index("p"), lax.axis_index("t")
    for c in range(CHIPS):
        rows = parts[c * TP + c // 4, 2 * HALF :, :].astype(F32)
        gains[c * 8 : (c + 1) * 8, :] = (rows + pltpu.roll(rows, 6, 0)) + pltpu.roll(rows, 4, 0)
    square = jnp.zeros((HALF, HD), F32)
    for c in range(2 * CHIPS):
        place = slice((c % 2) * HALF, (c % 2 + 1) * HALF)
        piece = parts[(c // 2) * TP, place, :].astype(F32)
        for t in range(1, TP):
            piece = piece + parts[(c // 2) * TP + t, place, :].astype(F32)
        mid[c * HALF : (c + 1) * HALF, :] = piece
        square = square + piece * piece
    scale = lax.rsqrt(jnp.sum(square, axis=1, keepdims=True) / D + EPSILON)
    mid_row[...] = mid[pl.ds(plane * 8 * HALF + chip, 8, stride=HALF), :]

    def normed_columns(c):
        return (mid[c * HALF : (c + 1) * HALF, :] * scale * gains[c // 2 * 8 + c % 2 : c // 2 * 8 + c % 2 + 1, :]).astype(BF16)

    normed = jnp.concatenate([normed_columns(c) for c in range(2 * CHIPS)], axis=1)

    def hidden_units(gate, up):
        over = (((1,), (1,)), ((), ()))
        gate_out = lax.dot_general(normed, gate[...], over, preferred_element_type=F32)
        up_out = lax.dot_general(normed, up[...], over, preferred_element_type=F32)
        return (gate_out / (1.0 + jnp.exp(-gate_out)) * up_out).astype(BF16)

    act0, act1 = hidden_units(gate0, up0), hidden_units(gate1, up1)
    wide = 512
    for n in range(D // wide):
        place = slice(n * wide, (n + 1) * wide)
        partial = jnp.dot(act0, down0[:, place], preferred_element_type=F32) + jnp.dot(
            act1, down1[:, place], preferred_element_type=F32
        )
        for i in range(wide // HD):
            c = n * (wide // HD) + i
            sums[pl.ds(c, HALF, stride=2 * CHIPS), :] = partial[:, i * HD : (i + 1) * HD]
    message[...] = sums[...].astype(BF16)


def sum_kernel(parts, mid_row, out):
    total = parts[0].astype(F32)
    for s in range(1, CHIPS * TP):
        total = total + parts[s].astype(F32)
    total = (mid_row[...] + total).astype(BF16)
    for r in range(8):
        out[:, r * HD : (r + 1) * HD] = total[r : r + 1, :]


def in_vmem(shape, dtype):
    return pltpu.VMEM(shape, dtype)


def stay(x):
    return pltpu.with_memory_space_constraint(x, pltpu.HBM)


def held(x):
    return pltpu.with_memory_space_constraint(x, pltpu.VMEM)


def call(kernel, out_shape, operands, scratch=(), far=(), pinned=(), limit=SMALL, cost=None):
    vmem = pl.BlockSpec(memory_space=pltpu.VMEM)
    specs = [pl.BlockSpec(memory_space=pl.ANY) if i in far else vmem for i in range(len(operands))]
    return pl.pallas_call(
        kernel,
        out_shape=out_shape,
        in_specs=specs,
        out_specs=jax.tree.map(lambda _: vmem, out_shape, is_leaf=lambda x: not isinstance(x, tuple)),
        scratch_shapes=list(scratch),
        compiler_params=pltpu.CompilerParams(vmem_limit_bytes=limit),
        cost_estimate=cost,
    )(*(stay(x) if i in pinned else x for i, x in enumerate(operands)))


def shards(
    hidden_in,
    query,
    new_key,
    new_value,
    cache_keys,
    cache_values,
    lengths,
    out_weight,
    norm_gain,
    w_gate,
    w_up,
    w_down,
):
    def other_core(x):
        return lax.ppermute(x, "k", [(0, 1), (1, 0)])

    w_gate, w_up = w_gate.T, w_up.T
    inputs = (query, hidden_in, new_key, new_value, lengths)
    message, own, limits = call(
        start_kernel,
        (in_vmem((SEQS, 16, HD), BF16), in_vmem((2, HEADS, HD), F32), in_vmem((SEQS, HD), jnp.int32)),
        (*inputs, cache_keys, cache_values),
        [
            *(pltpu.VMEM(x.shape, x.dtype) for x in inputs[:4]),
            pltpu.SMEM(lengths.shape, jnp.int32),
            pltpu.SemaphoreType.DMA((5,)),
        ],
        far=range(7),
        pinned=range(7),
    )
    gathered = lax.all_to_all(message, ("p", "k"), 0, 0, tiled=True)
    *exchanged, gathered = lax.optimization_barrier((out_weight, w_gate, w_up, w_down, gathered))
    other_out_weight, other_gate, other_up, other_down = map(other_core, exchanged)
    cache = held(cache_keys), held(cache_values)
    sent = call(
        other_kernel,
        in_vmem((MSG, HD), BF16),
        (limits, gathered, *cache),
        [pltpu.VMEM((ROWS, HD), F32), pltpu.VMEM((ROWS, HD), F32)],
    )
    came = other_core(sent)
    kept, kept_lse, hidden_part = call(
        kept_kernel,
        (in_vmem((ROWS, HD), F32), in_vmem((ROWS, HD), F32), in_vmem((2, HALF, HD), F32)),
        (limits, gathered, own, *cache),
        [pltpu.VMEM((SEQS * 16, HD), F32)],
    )
    blocks = call(merge_kernel, in_vmem((CHIPS, MSG, HD), BF16), (kept, kept_lse, came))
    blocks, other_gate, other_up, other_down, other_out_weight = lax.optimization_barrier(
        (blocks, other_gate, other_up, other_down, other_out_weight)
    )
    blocks = lax.all_to_all(blocks, "p", 0, 0, tiled=True)
    columns = call(
        project_kernel,
        in_vmem((CHIPS * TP, 2 * HALF + 8, HD), BF16),
        (blocks, hidden_part, norm_gain.reshape(8, HD), out_weight, other_out_weight),
    )
    columns = lax.all_to_all(columns, ("p", "t"), 0, 0, tiled=True)
    partial, mid_row = call(
        feed_kernel,
        (in_vmem((CHIPS * TP * 8, HD), BF16), in_vmem((8, HD), F32)),
        (columns, w_gate, w_up, other_gate, other_up, w_down, other_down),
        [
            pltpu.VMEM((2 * CHIPS * HALF, HD), F32),
            pltpu.VMEM((CHIPS * TP * 8, HD), F32),
            pltpu.VMEM((CHIPS * 8, HD), F32),
        ],
    )
    partial = lax.all_to_all(partial.reshape(CHIPS * TP, 8, HD), ("p", "t"), 0, 0, tiled=True)
    return call(sum_kernel, jax.ShapeDtypeStruct((1, 8 * HD), BF16), (partial, mid_row))


def solution(mesh):
    cut = Mesh(mesh.devices.reshape(CHIPS, 2, TP), ("p", "k", "t"))
    ctx, tp = ("p", "k"), "t"
    return jax.shard_map(
        shards,
        mesh=cut,
        in_specs=(
            P(ctx, tp),
            P(ctx, tp),
            P(ctx, tp),
            P(ctx, tp),
            P(None, ctx, tp),
            P(None, ctx, tp),
            P(),
            P(tp, ctx),
            P(tp),
            P(None, ("p", "k", "t")),
            P(None, ("p", "k", "t")),
            P(("p", "k", "t"), None),
        ),
        out_specs=P(ctx, tp),
        check_vma=False,
    )
```

```python
import functools
import math

import jax
import jax.numpy as jnp
from jax import lax
from jax.experimental import pallas as pl
from jax.experimental.pallas import tpu as pltpu
from jax.sharding import Mesh
from jax.sharding import PartitionSpec as P

D = 4096
HD = 128
EPSILON = 1e-05
MASKED = -1e30
F32 = jnp.float32
BF16 = jnp.bfloat16

CHIPS = 16
TP = 4
SEQS = 32
HALF = 16
HEADS = 8
GROUP = 8
ROWS = HEADS * HALF
MSG = ROWS + 8

SMALL = 8 * 1024 * 1024


def pack_lse(lse_of_head):
    lane = lax.broadcasted_iota(jnp.int32, (HALF, 128), 1)
    packed = jnp.zeros((HALF, 128), F32)
    for h in range(HEADS):
        for i, part in enumerate(addends(lse_of_head(h))):
            packed = jnp.where(lane == i * HEADS + h, part, packed)
    return (packed[:8] + pltpu.roll(packed[8:], 3 * HEADS, 1)).astype(BF16)


def unpack_lse(packed):
    packed = packed.astype(F32)
    packed = jnp.concatenate([packed, pltpu.roll(packed, 128 - 3 * HEADS, 1)], axis=0)
    return (packed + pltpu.roll(packed, 128 - HEADS, 1)) + pltpu.roll(packed, 128 - 2 * HEADS, 1)


def addends(x):
    high = x.astype(BF16).astype(F32)
    middle = (x - high).astype(BF16).astype(F32)
    return high, middle, x - high - middle


def copy_in(sources, targets, arrived):
    copies = [pltpu.make_async_copy(a, b, arrived.at[i]) for i, (a, b) in enumerate(zip(sources, targets))]
    for copy in copies:
        copy.start()
    return copies


def start_kernel(*refs):
    sources, (message, own, limits), landed, arrived = refs[:5], refs[7:10], refs[10:15], refs[15]
    for copy in copy_in(sources, landed, arrived):
        copy.wait()
    query, hidden, own_key, own_value, lengths = landed

    def rows(x):
        x = x[...].astype(F32)
        return jnp.concatenate([x[:, r * HD : (r + 1) * HD] for r in range(8)], axis=0)

    def heads(x):
        x = x[...].astype(F32)
        return jnp.concatenate([x[:, (h // 4) * HD : (h // 4 + 1) * HD] for h in range(HEADS)], axis=0)

    queries = rows(query)
    both = jnp.concatenate([queries, rows(hidden)], axis=0).astype(BF16)
    message[...] = jnp.broadcast_to(both[None], message.shape)
    score = jnp.sum(queries * heads(own_key), axis=1, keepdims=True) * (1.0 / math.sqrt(HD))
    own[0] = jnp.broadcast_to(score, (HEADS, HD))
    own[1] = heads(own_value)
    for b in range(SEQS):
        limits[b : b + 1, :] = jnp.full((1, HD), lengths[b], jnp.int32)


def attend(parity, limits, gathered, keys, values, outs, lses):
    chip, core = lax.axis_index("p"), lax.axis_index("k")
    ctx_dev = keys.shape[1]
    factor = 1.0 / math.sqrt(HD)
    head = lax.broadcasted_iota(jnp.int32, (HEADS, HD), 0)
    zero = jnp.zeros((HEADS, HD), BF16)
    places = (chip * 2 + core) * ctx_dev + lax.broadcasted_iota(jnp.int32, (HEADS, ctx_dev), 1)

    def score(b):
        query = gathered[b][:HEADS]
        wide = jnp.concatenate(
            [jnp.where(head < HEADS // 2, query, zero), jnp.where(head >= HEADS // 2, query, zero)], axis=1
        )
        return lax.dot_general(wide, keys[b], (((1,), (1,)), ((), ())), preferred_element_type=F32) * factor

    def soften(b, scores):
        limit = limits[pl.ds(b, 1), :]
        valid = places < jnp.concatenate([limit] * (ctx_dev // HD), axis=1)
        top = jnp.max(jnp.where(valid, scores, MASKED), axis=1, keepdims=True)
        weights = jnp.where(valid, jnp.exp(scores - top), 0.0).astype(BF16)
        return top, weights, jnp.sum(weights.astype(F32), axis=1, keepdims=True)

    def collect(b, top, weights, den):
        num = jnp.dot(weights, values[b], preferred_element_type=F32)
        num = jnp.where(head < HEADS // 2, num[:, :HD], num[:, HD:])
        some = den > 0.0
        safe = jnp.where(some, den, 1.0)
        return num / safe, jnp.where(some, top + jnp.log(safe), MASKED)

    for at in range(0, HALF, GROUP):
        sequences = [2 * j + parity for j in range(at, at + GROUP)]
        scores = [score(b) for b in sequences]
        softened = [soften(b, x) for b, x in zip(sequences, scores)]
        collected = [collect(b, *x) for b, x in zip(sequences, softened)]
        for i, (out, lse) in enumerate(collected):
            outs[pl.ds(at + i, HEADS, stride=HALF), :] = out
            lses[pl.ds(at + i, HEADS, stride=HALF), :] = jnp.broadcast_to(lse, (HEADS, HD))


def other_kernel(limits, gathered, keys, values, sent, outs, lses):
    attend(1 - lax.axis_index("k"), limits, gathered, keys, values, outs, lses)
    sent[:ROWS, :] = outs[...].astype(BF16)
    sent[ROWS:, :] = pack_lse(lambda h: lses[h * HALF : (h + 1) * HALF, :])


def kept_kernel(limits, gathered, own, keys, values, kept, kept_lse, hidden_part, outs, lses, rows):
    chip, core, plane = lax.axis_index("p"), lax.axis_index("k"), lax.axis_index("t")
    attend(core, limits, gathered, keys, values, outs, lses)
    fresh_score, value = own[0], own[1]
    place = pl.ds(chip, HEADS, stride=HALF)
    cached, block_lse = outs[place, :], lses[place, :]
    top = jnp.maximum(block_lse, fresh_score)
    keep, fresh = jnp.exp(block_lse - top), jnp.exp(fresh_score - top)
    total = keep + fresh
    outs[place, :] = (cached * keep + value * fresh) / total
    lses[place, :] = top + jnp.log(total)
    kept[...] = outs[:ROWS, :]
    kept_lse[...] = lses[:ROWS, :]
    rows[: SEQS * 16, :] = gathered[...].reshape(SEQS * 16, HD).astype(F32)
    column = core * 16 + HEADS + (chip % 4) * 2
    for i in range(2):
        part = rows[pl.ds(column + i, HALF, stride=32), :]
        hidden_part[i] = jnp.where(plane == chip // 4, part, 0.0)


def merge_kernel(kept, kept_lse, came, message):
    came_lse = unpack_lse(came[ROWS:, :])
    merged_lse = []
    for h in range(HEADS):
        place = slice(h * HALF, (h + 1) * HALF)
        mine = kept_lse[place, :]
        theirs = came_lse[:, h : h + 1]
        top = jnp.maximum(mine, theirs)
        left, right = jnp.exp(mine - top), jnp.exp(theirs - top)
        total = left + right
        block = (kept[place, :] * left + came[place, :].astype(F32) * right) / total
        message[:, place, :] = jnp.broadcast_to(block.astype(BF16)[None], (CHIPS, HALF, HD))
        merged_lse.append(top + jnp.log(total))
    packed = pack_lse(lambda h: merged_lse[h])
    message[:, ROWS:, :] = jnp.broadcast_to(packed[None], (CHIPS, 8, HD))


def project_kernel(blocks, hidden_part, gain, weight, other_weight, message):
    chip, core, plane = lax.axis_index("p"), lax.axis_index("k"), lax.axis_index("t")
    lse = []
    for s in range(CHIPS):
        lse.append(unpack_lse(blocks[s, ROWS:, :]))
    top = lse[0]
    for s in range(1, CHIPS):
        top = jnp.maximum(top, lse[s])
    share = [jnp.exp(x - top) for x in lse]
    total = share[0]
    for s in range(1, CHIPS):
        total = total + share[s]
    share = [x / total for x in share]
    columns = []
    for h in range(HEADS):
        place = slice(h * HALF, (h + 1) * HALF)
        acc = jnp.zeros((HALF, HD), F32)
        for s in range(CHIPS):
            acc = acc + share[s][:, h : h + 1] * blocks[s, place, :].astype(F32)
        columns.append(acc.astype(BF16))
    attention = jnp.concatenate(columns, axis=1)
    mine = jnp.dot(attention, weight[...], preferred_element_type=F32)
    other = jnp.dot(attention, other_weight[...], preferred_element_type=F32)
    low, high = jnp.where(core == 0, mine, other), jnp.where(core == 0, other, mine)
    for i, rows in enumerate((low, high)):
        rows = (rows + hidden_part[i]).astype(BF16)
        message[:, i * HALF : (i + 1) * HALF, :] = jnp.broadcast_to(rows[None], (CHIPS * TP, HALF, HD))
    rows = jnp.concatenate([*addends(gain[pl.ds((chip % 4) * 2, 2), :]), jnp.zeros((2, HD), F32)], axis=0)
    rows = jnp.where(plane == chip // 4, rows, 0.0).astype(BF16)
    message[:, 2 * HALF :, :] = jnp.broadcast_to(rows[None], (CHIPS * TP, 8, HD))


def feed_kernel(
    parts, gate0, up0, gate1, up1, down0, down1, message, mid_row, mid, sums, gains
):
    chip, plane = lax.axis_index("p"), lax.axis_index("t")
    for c in range(CHIPS):
        rows = parts[c * TP + c // 4, 2 * HALF :, :].astype(F32)
        gains[c * 8 : (c + 1) * 8, :] = (rows + pltpu.roll(rows, 6, 0)) + pltpu.roll(rows, 4, 0)
    square = jnp.zeros((HALF, HD), F32)
    for c in range(2 * CHIPS):
        place = slice((c % 2) * HALF, (c % 2 + 1) * HALF)
        piece = parts[(c // 2) * TP, place, :].astype(F32)
        for t in range(1, TP):
            piece = piece + parts[(c // 2) * TP + t, place, :].astype(F32)
        mid[c * HALF : (c + 1) * HALF, :] = piece
        square = square + piece * piece
    scale = lax.rsqrt(jnp.sum(square, axis=1, keepdims=True) / D + EPSILON)
    mid_row[...] = mid[pl.ds(plane * 8 * HALF + chip, 8, stride=HALF), :]

    def normed_columns(c):
        return (mid[c * HALF : (c + 1) * HALF, :] * scale * gains[c // 2 * 8 + c % 2 : c // 2 * 8 + c % 2 + 1, :]).astype(BF16)

    normed = jnp.concatenate([normed_columns(c) for c in range(2 * CHIPS)], axis=1)

    def hidden_units(gate, up):
        over = (((1,), (1,)), ((), ()))
        gate_out = lax.dot_general(normed, gate[...], over, preferred_element_type=F32)
        up_out = lax.dot_general(normed, up[...], over, preferred_element_type=F32)
        return (gate_out / (1.0 + jnp.exp(-gate_out)) * up_out).astype(BF16)

    act0, act1 = hidden_units(gate0, up0), hidden_units(gate1, up1)
    wide = 512
    for n in range(D // wide):
        place = slice(n * wide, (n + 1) * wide)
        partial = jnp.dot(act0, down0[:, place], preferred_element_type=F32) + jnp.dot(
            act1, down1[:, place], preferred_element_type=F32
        )
        for i in range(wide // HD):
            c = n * (wide // HD) + i
            sums[pl.ds(c, HALF, stride=2 * CHIPS), :] = partial[:, i * HD : (i + 1) * HD]
    message[...] = sums[...].astype(BF16)


def sum_kernel(parts, mid_row, out):
    total = parts[0].astype(F32)
    for s in range(1, CHIPS * TP):
        total = total + parts[s].astype(F32)
    total = (mid_row[...] + total).astype(BF16)
    for r in range(8):
        out[:, r * HD : (r + 1) * HD] = total[r : r + 1, :]


def in_vmem(shape, dtype):
    return pltpu.VMEM(shape, dtype)


def stay(x):
    return pltpu.with_memory_space_constraint(x, pltpu.HBM)


def held(x):
    return pltpu.with_memory_space_constraint(x, pltpu.VMEM)


def call(kernel, out_shape, operands, scratch=(), far=(), pinned=(), limit=SMALL, cost=None):
    vmem = pl.BlockSpec(memory_space=pltpu.VMEM)
    specs = [pl.BlockSpec(memory_space=pl.ANY) if i in far else vmem for i in range(len(operands))]
    return pl.pallas_call(
        kernel,
        out_shape=out_shape,
        in_specs=specs,
        out_specs=jax.tree.map(lambda _: vmem, out_shape, is_leaf=lambda x: not isinstance(x, tuple)),
        scratch_shapes=list(scratch),
        compiler_params=pltpu.CompilerParams(vmem_limit_bytes=limit),
        cost_estimate=cost,
    )(*(stay(x) if i in pinned else x for i, x in enumerate(operands)))


def shards(
    hidden_in,
    query,
    new_key,
    new_value,
    cache_keys,
    cache_values,
    lengths,
    out_weight,
    norm_gain,
    w_gate,
    w_up,
    w_down,
):
    def other_core(x):
        return lax.ppermute(x, "k", [(0, 1), (1, 0)])

    w_gate, w_up = w_gate.T, w_up.T
    inputs = (query, hidden_in, new_key, new_value, lengths)
    message, own, limits = call(
        start_kernel,
        (in_vmem((SEQS, 16, HD), BF16), in_vmem((2, HEADS, HD), F32), in_vmem((SEQS, HD), jnp.int32)),
        (*inputs, cache_keys, cache_values),
        [
            *(pltpu.VMEM(x.shape, x.dtype) for x in inputs[:4]),
            pltpu.SMEM(lengths.shape, jnp.int32),
            pltpu.SemaphoreType.DMA((5,)),
        ],
        far=range(7),
        pinned=range(7),
    )
    gathered = lax.all_to_all(message, ("p", "k"), 0, 0, tiled=True)
    *exchanged, gathered = lax.optimization_barrier((out_weight, w_gate, w_up, w_down, gathered))
    other_out_weight, other_gate, other_up, other_down = map(other_core, exchanged)
    cache = held(cache_keys), held(cache_values)
    sent = call(
        other_kernel,
        in_vmem((MSG, HD), BF16),
        (limits, gathered, *cache),
        [pltpu.VMEM((ROWS, HD), F32), pltpu.VMEM((ROWS, HD), F32)],
    )
    came = other_core(sent)
    kept, kept_lse, hidden_part = call(
        kept_kernel,
        (in_vmem((ROWS, HD), F32), in_vmem((ROWS, HD), F32), in_vmem((2, HALF, HD), F32)),
        (limits, gathered, own, *cache),
        [
            pltpu.VMEM((ROWS + HALF, HD), F32),
            pltpu.VMEM((ROWS + HALF, HD), F32),
            pltpu.VMEM((SEQS * 16 + 32, HD), F32),
        ],
    )
    blocks = call(merge_kernel, in_vmem((CHIPS, MSG, HD), BF16), (kept, kept_lse, came))
    blocks, other_gate, other_up, other_down, other_out_weight = lax.optimization_barrier(
        (blocks, other_gate, other_up, other_down, other_out_weight)
    )
    blocks = lax.all_to_all(blocks, "p", 0, 0, tiled=True)
    columns = call(
        project_kernel,
        in_vmem((CHIPS * TP, 2 * HALF + 8, HD), BF16),
        (blocks, hidden_part, norm_gain.reshape(8, HD), out_weight, other_out_weight),
    )
    columns = lax.all_to_all(columns, ("p", "t"), 0, 0, tiled=True)
    partial, mid_row = call(
        feed_kernel,
        (in_vmem((CHIPS * TP * 8, HD), BF16), in_vmem((8, HD), F32)),
        (columns, w_gate, w_up, other_gate, other_up, w_down, other_down),
        [
            pltpu.VMEM((2 * CHIPS * HALF + HALF, HD), F32),
            pltpu.VMEM((CHIPS * TP * 8, HD), F32),
            pltpu.VMEM((CHIPS * 8, HD), F32),
        ],
    )
    partial = lax.all_to_all(partial.reshape(CHIPS * TP, 8, HD), ("p", "t"), 0, 0, tiled=True)
    return call(sum_kernel, jax.ShapeDtypeStruct((1, 8 * HD), BF16), (partial, mid_row))


def solution(mesh):
    cut = Mesh(mesh.devices.reshape(CHIPS, 2, TP), ("p", "k", "t"))
    ctx, tp = ("p", "k"), "t"
    return jax.shard_map(
        shards,
        mesh=cut,
        in_specs=(
            P(ctx, tp),
            P(ctx, tp),
            P(ctx, tp),
            P(ctx, tp),
            P(None, ctx, tp),
            P(None, ctx, tp),
            P(),
            P(tp, ctx),
            P(tp),
            P(None, ("p", "k", "t")),
            P(None, ("p", "k", "t")),
            P(("p", "k", "t"), None),
        ),
        out_specs=P(ctx, tp),
        check_vma=False,
    )
```

```python
import functools
import math

import jax
import jax.numpy as jnp
from jax import lax
from jax.experimental import pallas as pl
from jax.experimental.pallas import tpu as pltpu
from jax.sharding import Mesh
from jax.sharding import PartitionSpec as P

D = 4096
HD = 128
EPSILON = 1e-05
MASKED = -1e30
F32 = jnp.float32
BF16 = jnp.bfloat16

CHIPS = 16
TP = 4
SEQS = 32
HALF = 16
HEADS = 8
GROUP = 8
ROWS = HEADS * HALF
MSG = ROWS + 8

SMALL = 8 * 1024 * 1024


def pack_lse(lse_of_head):
    lane = lax.broadcasted_iota(jnp.int32, (HALF, 128), 1)
    packed = jnp.zeros((HALF, 128), F32)
    for h in range(HEADS):
        for i, part in enumerate(addends(lse_of_head(h))):
            packed = jnp.where(lane == i * HEADS + h, part, packed)
    return (packed[:8] + pltpu.roll(packed[8:], 3 * HEADS, 1)).astype(BF16)


def unpack_lse(packed):
    packed = packed.astype(F32)
    packed = jnp.concatenate([packed, pltpu.roll(packed, 128 - 3 * HEADS, 1)], axis=0)
    return (packed + pltpu.roll(packed, 128 - HEADS, 1)) + pltpu.roll(packed, 128 - 2 * HEADS, 1)


def addends(x):
    high = x.astype(BF16).astype(F32)
    middle = (x - high).astype(BF16).astype(F32)
    return high, middle, x - high - middle


def copy_in(sources, targets, arrived):
    copies = [pltpu.make_async_copy(a, b, arrived.at[i]) for i, (a, b) in enumerate(zip(sources, targets))]
    for copy in copies:
        copy.start()
    return copies


def start_kernel(*refs):
    sources, (message, own, limits), landed, arrived = refs[:5], refs[7:10], refs[10:15], refs[15]
    for copy in copy_in(sources, landed, arrived):
        copy.wait()
    query, hidden, own_key, own_value, lengths = landed

    def rows(x):
        x = x[...].astype(F32)
        return jnp.concatenate([x[:, r * HD : (r + 1) * HD] for r in range(8)], axis=0)

    def heads(x):
        x = x[...].astype(F32)
        return jnp.concatenate([x[:, (h // 4) * HD : (h // 4 + 1) * HD] for h in range(HEADS)], axis=0)

    queries = rows(query)
    both = jnp.concatenate([queries, rows(hidden)], axis=0).astype(BF16)
    message[...] = jnp.broadcast_to(both[None], message.shape)
    score = jnp.sum(queries * heads(own_key), axis=1, keepdims=True) * (1.0 / math.sqrt(HD))
    own[0] = jnp.broadcast_to(score, (HEADS, HD))
    own[1] = heads(own_value)
    for b in range(SEQS):
        limits[b : b + 1, :] = jnp.full((1, HD), lengths[b], jnp.int32)


def attend(parity, limits, gathered, keys, values, outs, lses):
    chip, core = lax.axis_index("p"), lax.axis_index("k")
    ctx_dev = keys.shape[1]
    factor = 1.0 / math.sqrt(HD)
    head = lax.broadcasted_iota(jnp.int32, (HEADS, HD), 0)
    zero = jnp.zeros((HEADS, HD), BF16)
    places = (chip * 2 + core) * ctx_dev + lax.broadcasted_iota(jnp.int32, (HEADS, ctx_dev), 1)

    def score(b):
        query = gathered[b][:HEADS]
        wide = jnp.concatenate(
            [jnp.where(head < HEADS // 2, query, zero), jnp.where(head >= HEADS // 2, query, zero)], axis=1
        )
        return lax.dot_general(wide, keys[b], (((1,), (1,)), ((), ())), preferred_element_type=F32) * factor

    def soften(b, scores):
        limit = limits[pl.ds(b, 1), :]
        valid = places < jnp.concatenate([limit] * (ctx_dev // HD), axis=1)
        top = jnp.max(jnp.where(valid, scores, MASKED), axis=1, keepdims=True)
        weights = jnp.where(valid, jnp.exp(scores - top), 0.0).astype(BF16)
        return top, weights, jnp.sum(weights.astype(F32), axis=1, keepdims=True)

    def collect(b, top, weights, den):
        num = jnp.dot(weights, values[b], preferred_element_type=F32)
        num = jnp.where(head < HEADS // 2, num[:, :HD], num[:, HD:])
        some = den > 0.0
        safe = jnp.where(some, den, 1.0)
        return num / safe, jnp.where(some, top + jnp.log(safe), MASKED)

    for at in range(0, HALF, GROUP):
        sequences = [2 * j + parity for j in range(at, at + GROUP)]
        scores = [score(b) for b in sequences]
        softened = [soften(b, x) for b, x in zip(sequences, scores)]
        collected = [collect(b, *x) for b, x in zip(sequences, softened)]
        for i, (out, lse) in enumerate(collected):
            outs[pl.ds(at + i, HEADS, stride=HALF), :] = out
            lses[pl.ds(at + i, HEADS, stride=HALF), :] = jnp.broadcast_to(lse, (HEADS, HD))


def other_kernel(limits, gathered, keys, values, sent, outs, lses):
    attend(1 - lax.axis_index("k"), limits, gathered, keys, values, outs, lses)
    sent[:ROWS, :] = outs[...].astype(BF16)
    sent[ROWS:, :] = pack_lse(lambda h: lses[h * HALF : (h + 1) * HALF, :])


def kept_kernel(limits, gathered, own, keys, values, kept, kept_lse, hidden_part, outs, lses, rows):
    chip, core, plane = lax.axis_index("p"), lax.axis_index("k"), lax.axis_index("t")
    attend(core, limits, gathered, keys, values, outs, lses)
    fresh_score, value = own[0], own[1]
    place = pl.ds(chip, HEADS, stride=HALF)
    cached, block_lse = outs[place, :], lses[place, :]
    top = jnp.maximum(block_lse, fresh_score)
    keep, fresh = jnp.exp(block_lse - top), jnp.exp(fresh_score - top)
    total = keep + fresh
    outs[place, :] = (cached * keep + value * fresh) / total
    lses[place, :] = top + jnp.log(total)
    kept[...] = outs[:ROWS, :]
    kept_lse[...] = lses[:ROWS, :]
    rows[: SEQS * 16, :] = gathered[...].reshape(SEQS * 16, HD).astype(F32)
    column = core * 16 + HEADS + (chip % 4) * 2
    for i in range(2):
        part = rows[pl.ds(column + i, HALF, stride=32), :]
        hidden_part[i] = jnp.where(plane == chip // 4, part, 0.0)


def merge_kernel(kept, kept_lse, came, message):
    came_lse = unpack_lse(came[ROWS:, :])
    merged_lse = []
    for h in range(HEADS):
        place = slice(h * HALF, (h + 1) * HALF)
        mine = kept_lse[place, :]
        theirs = came_lse[:, h : h + 1]
        top = jnp.maximum(mine, theirs)
        left, right = jnp.exp(mine - top), jnp.exp(theirs - top)
        total = left + right
        block = (kept[place, :] * left + came[place, :].astype(F32) * right) / total
        message[:, place, :] = jnp.broadcast_to(block.astype(BF16)[None], (CHIPS, HALF, HD))
        merged_lse.append(top + jnp.log(total))
    packed = pack_lse(lambda h: merged_lse[h])
    message[:, ROWS:, :] = jnp.broadcast_to(packed[None], (CHIPS, 8, HD))


def project_kernel(blocks, hidden_part, gain, weight, other_weight, message):
    chip, core, plane = lax.axis_index("p"), lax.axis_index("k"), lax.axis_index("t")
    lse = []
    for s in range(CHIPS):
        lse.append(unpack_lse(blocks[s, ROWS:, :]))
    top = lse[0]
    for s in range(1, CHIPS):
        top = jnp.maximum(top, lse[s])
    share = [jnp.exp(x - top) for x in lse]
    total = share[0]
    for s in range(1, CHIPS):
        total = total + share[s]
    share = [x / total for x in share]
    columns = []
    for h in range(HEADS):
        place = slice(h * HALF, (h + 1) * HALF)
        acc = jnp.zeros((HALF, HD), F32)
        for s in range(CHIPS):
            acc = acc + share[s][:, h : h + 1] * blocks[s, place, :].astype(F32)
        columns.append(acc.astype(BF16))
    attention = jnp.concatenate(columns, axis=1)
    mine = jnp.dot(attention, weight[...], preferred_element_type=F32)
    other = jnp.dot(attention, other_weight[...], preferred_element_type=F32)
    low, high = jnp.where(core == 0, mine, other), jnp.where(core == 0, other, mine)
    for i, rows in enumerate((low, high)):
        rows = (rows + hidden_part[i]).astype(BF16)
        message[:, i * HALF : (i + 1) * HALF, :] = jnp.broadcast_to(rows[None], (CHIPS * TP, HALF, HD))
    rows = jnp.concatenate([*addends(gain[pl.ds((chip % 4) * 2, 2), :]), jnp.zeros((2, HD), F32)], axis=0)
    rows = jnp.where(plane == chip // 4, rows, 0.0).astype(BF16)
    message[:, 2 * HALF :, :] = jnp.broadcast_to(rows[None], (CHIPS * TP, 8, HD))


def feed_kernel(
    parts, gate0, up0, gate1, up1, down0, down1, message, mid_row, mid, sums, gains
):
    chip, plane = lax.axis_index("p"), lax.axis_index("t")
    for c in range(CHIPS):
        rows = parts[c * TP + c // 4, 2 * HALF :, :].astype(F32)
        gains[c * 8 : (c + 1) * 8, :] = (rows + pltpu.roll(rows, 6, 0)) + pltpu.roll(rows, 4, 0)
    square = jnp.zeros((HALF, HD), F32)
    for c in range(2 * CHIPS):
        place = slice((c % 2) * HALF, (c % 2 + 1) * HALF)
        piece = parts[(c // 2) * TP, place, :].astype(F32)
        for t in range(1, TP):
            piece = piece + parts[(c // 2) * TP + t, place, :].astype(F32)
        mid[c * HALF : (c + 1) * HALF, :] = piece
        square = square + piece * piece
    scale = lax.rsqrt(jnp.sum(square, axis=1, keepdims=True) / D + EPSILON)
    mid_row[...] = mid[pl.ds(plane * 8 * HALF + chip, 8, stride=HALF), :]

    def normed_columns(c):
        return (mid[c * HALF : (c + 1) * HALF, :] * gains[c // 2 * 8 + c % 2 : c // 2 * 8 + c % 2 + 1, :]).astype(BF16)

    normed = jnp.concatenate([normed_columns(c) for c in range(2 * CHIPS)], axis=1)

    def hidden_units(gate, up):
        over = (((1,), (1,)), ((), ()))
        gate_out = lax.dot_general(normed, gate[...], over, preferred_element_type=F32)
        up_out = lax.dot_general(normed, up[...], over, preferred_element_type=F32)
        gate_out, up_out = gate_out * scale, up_out * scale
        return (gate_out / (1.0 + jnp.exp(-gate_out)) * up_out).astype(BF16)

    act0, act1 = hidden_units(gate0, up0), hidden_units(gate1, up1)
    wide = 512
    for n in range(D // wide):
        place = slice(n * wide, (n + 1) * wide)
        partial = jnp.dot(act0, down0[:, place], preferred_element_type=F32) + jnp.dot(
            act1, down1[:, place], preferred_element_type=F32
        )
        for i in range(wide // HD):
            c = n * (wide // HD) + i
            sums[pl.ds(c, HALF, stride=2 * CHIPS), :] = partial[:, i * HD : (i + 1) * HD]
    message[...] = sums[...].astype(BF16)


def sum_kernel(parts, mid_row, out):
    total = parts[0].astype(F32)
    for s in range(1, CHIPS * TP):
        total = total + parts[s].astype(F32)
    total = (mid_row[...] + total).astype(BF16)
    for r in range(8):
        out[:, r * HD : (r + 1) * HD] = total[r : r + 1, :]


def in_vmem(shape, dtype):
    return pltpu.VMEM(shape, dtype)


def stay(x):
    return pltpu.with_memory_space_constraint(x, pltpu.HBM)


def held(x):
    return pltpu.with_memory_space_constraint(x, pltpu.VMEM)


def call(kernel, out_shape, operands, scratch=(), far=(), pinned=(), limit=SMALL, cost=None):
    vmem = pl.BlockSpec(memory_space=pltpu.VMEM)
    specs = [pl.BlockSpec(memory_space=pl.ANY) if i in far else vmem for i in range(len(operands))]
    return pl.pallas_call(
        kernel,
        out_shape=out_shape,
        in_specs=specs,
        out_specs=jax.tree.map(lambda _: vmem, out_shape, is_leaf=lambda x: not isinstance(x, tuple)),
        scratch_shapes=list(scratch),
        compiler_params=pltpu.CompilerParams(vmem_limit_bytes=limit),
        cost_estimate=cost,
    )(*(stay(x) if i in pinned else x for i, x in enumerate(operands)))


def shards(
    hidden_in,
    query,
    new_key,
    new_value,
    cache_keys,
    cache_values,
    lengths,
    out_weight,
    norm_gain,
    w_gate,
    w_up,
    w_down,
):
    def other_core(x):
        return lax.ppermute(x, "k", [(0, 1), (1, 0)])

    w_gate, w_up = w_gate.T, w_up.T
    inputs = (query, hidden_in, new_key, new_value, lengths)
    message, own, limits = call(
        start_kernel,
        (in_vmem((SEQS, 16, HD), BF16), in_vmem((2, HEADS, HD), F32), in_vmem((SEQS, HD), jnp.int32)),
        (*inputs, cache_keys, cache_values),
        [
            *(pltpu.VMEM(x.shape, x.dtype) for x in inputs[:4]),
            pltpu.SMEM(lengths.shape, jnp.int32),
            pltpu.SemaphoreType.DMA((5,)),
        ],
        far=range(7),
        pinned=range(7),
    )
    gathered = lax.all_to_all(message, ("p", "k"), 0, 0, tiled=True)
    *exchanged, gathered = lax.optimization_barrier((out_weight, w_gate, w_up, w_down, gathered))
    other_out_weight, other_gate, other_up, other_down = map(other_core, exchanged)
    cache = held(cache_keys), held(cache_values)
    sent = call(
        other_kernel,
        in_vmem((MSG, HD), BF16),
        (limits, gathered, *cache),
        [pltpu.VMEM((ROWS, HD), F32), pltpu.VMEM((ROWS, HD), F32)],
    )
    came = other_core(sent)
    kept, kept_lse, hidden_part = call(
        kept_kernel,
        (in_vmem((ROWS, HD), F32), in_vmem((ROWS, HD), F32), in_vmem((2, HALF, HD), F32)),
        (limits, gathered, own, *cache),
        [
            pltpu.VMEM((ROWS + HALF, HD), F32),
            pltpu.VMEM((ROWS + HALF, HD), F32),
            pltpu.VMEM((SEQS * 16 + 32, HD), F32),
        ],
    )
    blocks = call(merge_kernel, in_vmem((CHIPS, MSG, HD), BF16), (kept, kept_lse, came))
    blocks, other_gate, other_up, other_out_weight = lax.optimization_barrier(
        (blocks, other_gate, other_up, other_out_weight)
    )
    blocks = lax.all_to_all(blocks, "p", 0, 0, tiled=True)
    columns = call(
        project_kernel,
        in_vmem((CHIPS * TP, 2 * HALF + 8, HD), BF16),
        (blocks, hidden_part, norm_gain.reshape(8, HD), out_weight, other_out_weight),
    )
    columns, other_down = lax.optimization_barrier((columns, other_down))
    columns = lax.all_to_all(columns, ("p", "t"), 0, 0, tiled=True)
    partial, mid_row = call(
        feed_kernel,
        (in_vmem((CHIPS * TP * 8, HD), BF16), in_vmem((8, HD), F32)),
        (columns, w_gate, w_up, other_gate, other_up, w_down, other_down),
        [
            pltpu.VMEM((2 * CHIPS * HALF + HALF, HD), F32),
            pltpu.VMEM((CHIPS * TP * 8, HD), F32),
            pltpu.VMEM((CHIPS * 8, HD), F32),
        ],
    )
    partial = lax.all_to_all(partial.reshape(CHIPS * TP, 8, HD), ("p", "t"), 0, 0, tiled=True)
    return call(sum_kernel, jax.ShapeDtypeStruct((1, 8 * HD), BF16), (partial, mid_row))


def solution(mesh):
    cut = Mesh(mesh.devices.reshape(CHIPS, 2, TP), ("p", "k", "t"))
    ctx, tp = ("p", "k"), "t"
    return jax.shard_map(
        shards,
        mesh=cut,
        in_specs=(
            P(ctx, tp),
            P(ctx, tp),
            P(ctx, tp),
            P(ctx, tp),
            P(None, ctx, tp),
            P(None, ctx, tp),
            P(),
            P(tp, ctx),
            P(tp),
            P(None, ("p", "k", "t")),
            P(None, ("p", "k", "t")),
            P(("p", "k", "t"), None),
        ),
        out_specs=P(ctx, tp),
        check_vma=False,
    )
```

```python
import functools
import math

import jax
import jax.numpy as jnp
from jax import lax
from jax.experimental import pallas as pl
from jax.experimental.pallas import tpu as pltpu
from jax.sharding import Mesh
from jax.sharding import PartitionSpec as P

D = 4096
HD = 128
EPSILON = 1e-05
MASKED = -1e30
F32 = jnp.float32
BF16 = jnp.bfloat16

CHIPS = 16
TP = 4
SEQS = 32
HALF = 16
HEADS = 8
GROUP = 8
ROWS = HEADS * HALF
MSG = ROWS + 8

SMALL = 8 * 1024 * 1024


def pack_lse(lse_of_head):
    lane = lax.broadcasted_iota(jnp.int32, (HALF, 128), 1)
    packed = jnp.zeros((HALF, 128), F32)
    for h in range(HEADS):
        for i, part in enumerate(addends(lse_of_head(h))):
            packed = jnp.where(lane == i * HEADS + h, part, packed)
    return (packed[:8] + pltpu.roll(packed[8:], 3 * HEADS, 1)).astype(BF16)


def unpack_lse(packed):
    packed = packed.astype(F32)
    packed = jnp.concatenate([packed, pltpu.roll(packed, 128 - 3 * HEADS, 1)], axis=0)
    return (packed + pltpu.roll(packed, 128 - HEADS, 1)) + pltpu.roll(packed, 128 - 2 * HEADS, 1)


def addends(x):
    high = x.astype(BF16).astype(F32)
    middle = (x - high).astype(BF16).astype(F32)
    return high, middle, x - high - middle


def copy_in(sources, targets, arrived):
    copies = [pltpu.make_async_copy(a, b, arrived.at[i]) for i, (a, b) in enumerate(zip(sources, targets))]
    for copy in copies:
        copy.start()
    return copies


def start_kernel(*refs):
    sources, (message, own, limits), landed, arrived = refs[:5], refs[7:10], refs[10:15], refs[15]
    for copy in copy_in(sources, landed, arrived):
        copy.wait()
    query, hidden, own_key, own_value, lengths = landed

    def rows(x):
        x = x[...].astype(F32)
        return jnp.concatenate([x[:, r * HD : (r + 1) * HD] for r in range(8)], axis=0)

    def heads(x):
        x = x[...].astype(F32)
        return jnp.concatenate([x[:, (h // 4) * HD : (h // 4 + 1) * HD] for h in range(HEADS)], axis=0)

    queries = rows(query)
    both = jnp.concatenate([queries, rows(hidden)], axis=0).astype(BF16)
    message[...] = jnp.broadcast_to(both[None], message.shape)
    score = jnp.sum(queries * heads(own_key), axis=1, keepdims=True) * (1.0 / math.sqrt(HD))
    own[0] = jnp.broadcast_to(score, (HEADS, HD))
    own[1] = heads(own_value)
    for b in range(SEQS):
        limits[b : b + 1, :] = jnp.full((1, HD), lengths[b], jnp.int32)


def attend(parity, limits, gathered, keys, values, outs, lses):
    chip, core = lax.axis_index("p"), lax.axis_index("k")
    ctx_dev = keys.shape[1]
    factor = 1.0 / math.sqrt(HD)
    head = lax.broadcasted_iota(jnp.int32, (HEADS, HD), 0)
    zero = jnp.zeros((HEADS, HD), BF16)
    places = (chip * 2 + core) * ctx_dev + lax.broadcasted_iota(jnp.int32, (HEADS, ctx_dev), 1)

    def score(b):
        query = gathered[b][:HEADS]
        wide = jnp.concatenate(
            [jnp.where(head < HEADS // 2, query, zero), jnp.where(head >= HEADS // 2, query, zero)], axis=1
        )
        return lax.dot_general(wide, keys[b], (((1,), (1,)), ((), ())), preferred_element_type=F32) * factor

    def soften(b, scores):
        limit = limits[pl.ds(b, 1), :]
        valid = places < jnp.concatenate([limit] * (ctx_dev // HD), axis=1)
        top = jnp.max(jnp.where(valid, scores, MASKED), axis=1, keepdims=True)
        weights = jnp.where(valid, jnp.exp(scores - top), 0.0).astype(BF16)
        return top, weights, jnp.sum(weights.astype(F32), axis=1, keepdims=True)

    def collect(b, top, weights, den):
        num = jnp.dot(weights, values[b], preferred_element_type=F32)
        num = jnp.where(head < HEADS // 2, num[:, :HD], num[:, HD:])
        some = den > 0.0
        safe = jnp.where(some, den, 1.0)
        return num / safe, jnp.where(some, top + jnp.log(safe), MASKED)

    for at in range(0, HALF, GROUP):
        sequences = [2 * j + parity for j in range(at, at + GROUP)]
        scores = [score(b) for b in sequences]
        softened = [soften(b, x) for b, x in zip(sequences, scores)]
        collected = [collect(b, *x) for b, x in zip(sequences, softened)]
        for i, (out, lse) in enumerate(collected):
            outs[pl.ds(at + i, HEADS, stride=HALF), :] = out
            lses[pl.ds(at + i, HEADS, stride=HALF), :] = jnp.broadcast_to(lse, (HEADS, HD))


def other_kernel(limits, gathered, keys, values, sent, outs, lses):
    attend(1 - lax.axis_index("k"), limits, gathered, keys, values, outs, lses)
    sent[:ROWS, :] = outs[...].astype(BF16)
    sent[ROWS:, :] = pack_lse(lambda h: lses[h * HALF : (h + 1) * HALF, :])


def kept_kernel(limits, gathered, own, keys, values, kept, kept_lse, hidden_part, outs, lses, rows):
    chip, core, plane = lax.axis_index("p"), lax.axis_index("k"), lax.axis_index("t")
    attend(core, limits, gathered, keys, values, outs, lses)
    fresh_score, value = own[0], own[1]
    place = pl.ds(chip, HEADS, stride=HALF)
    cached, block_lse = outs[place, :], lses[place, :]
    top = jnp.maximum(block_lse, fresh_score)
    keep, fresh = jnp.exp(block_lse - top), jnp.exp(fresh_score - top)
    total = keep + fresh
    outs[place, :] = (cached * keep + value * fresh) / total
    lses[place, :] = top + jnp.log(total)
    kept[...] = outs[:ROWS, :]
    kept_lse[...] = lses[:ROWS, :]
    rows[: SEQS * 16, :] = gathered[...].reshape(SEQS * 16, HD).astype(F32)
    column = core * 16 + HEADS + (chip % 4) * 2
    for i in range(2):
        part = rows[pl.ds(column + i, HALF, stride=32), :]
        hidden_part[i] = jnp.where(plane == chip // 4, part, 0.0)


def merge_kernel(kept, kept_lse, came, message):
    came_lse = unpack_lse(came[ROWS:, :])
    merged_lse = []
    for h in range(HEADS):
        place = slice(h * HALF, (h + 1) * HALF)
        mine = kept_lse[place, :]
        theirs = came_lse[:, h : h + 1]
        top = jnp.maximum(mine, theirs)
        left, right = jnp.exp(mine - top), jnp.exp(theirs - top)
        total = left + right
        block = (kept[place, :] * left + came[place, :].astype(F32) * right) / total
        message[:, place, :] = jnp.broadcast_to(block.astype(BF16)[None], (CHIPS, HALF, HD))
        merged_lse.append(top + jnp.log(total))
    packed = pack_lse(lambda h: merged_lse[h])
    message[:, ROWS:, :] = jnp.broadcast_to(packed[None], (CHIPS, 8, HD))


def project_kernel(blocks, hidden_part, gain, weight, other_weight, message):
    chip, core, plane = lax.axis_index("p"), lax.axis_index("k"), lax.axis_index("t")
    lse = []
    for s in range(CHIPS):
        lse.append(unpack_lse(blocks[s, ROWS:, :]))
    top = lse[0]
    for s in range(1, CHIPS):
        top = jnp.maximum(top, lse[s])
    share = [jnp.exp(x - top) for x in lse]
    total = share[0]
    for s in range(1, CHIPS):
        total = total + share[s]
    share = [x / total for x in share]
    columns = []
    for h in range(HEADS):
        place = slice(h * HALF, (h + 1) * HALF)
        acc = jnp.zeros((HALF, HD), F32)
        for s in range(CHIPS):
            acc = acc + share[s][:, h : h + 1] * blocks[s, place, :].astype(F32)
        columns.append(acc.astype(BF16))
    attention = jnp.concatenate(columns, axis=1)
    mine = jnp.dot(attention, weight[...], preferred_element_type=F32)
    other = jnp.dot(attention, other_weight[...], preferred_element_type=F32)
    low, high = jnp.where(core == 0, mine, other), jnp.where(core == 0, other, mine)
    for i, rows in enumerate((low, high)):
        rows = (rows + hidden_part[i]).astype(BF16)
        message[:, i * HALF : (i + 1) * HALF, :] = jnp.broadcast_to(rows[None], (CHIPS * TP, HALF, HD))
    rows = jnp.concatenate([*addends(gain[pl.ds((chip % 4) * 2, 2), :]), jnp.zeros((2, HD), F32)], axis=0)
    rows = jnp.where(plane == chip // 4, rows, 0.0).astype(BF16)
    message[:, 2 * HALF :, :] = jnp.broadcast_to(rows[None], (CHIPS * TP, 8, HD))


def feed_kernel(
    parts, gate0, up0, gate1, up1, down0, down1, message, mid_row, mid, sums, gains
):
    chip, plane = lax.axis_index("p"), lax.axis_index("t")
    for c in range(CHIPS):
        rows = parts[c * TP + c // 4, 2 * HALF :, :].astype(F32)
        gains[c * 8 : (c + 1) * 8, :] = (rows + pltpu.roll(rows, 6, 0)) + pltpu.roll(rows, 4, 0)
    square = jnp.zeros((HALF, HD), F32)
    for c in range(2 * CHIPS):
        place = slice((c % 2) * HALF, (c % 2 + 1) * HALF)
        piece = parts[(c // 2) * TP, place, :].astype(F32)
        for t in range(1, TP):
            piece = piece + parts[(c // 2) * TP + t, place, :].astype(F32)
        mid[c * HALF : (c + 1) * HALF, :] = piece
        square = square + piece * piece
    scale = lax.rsqrt(jnp.sum(square, axis=1, keepdims=True) / D + EPSILON)
    mid_row[...] = mid[pl.ds(plane * 8 * HALF + chip, 8, stride=HALF), :]

    def normed_columns(c):
        return (mid[c * HALF : (c + 1) * HALF, :] * scale * gains[c // 2 * 8 + c % 2 : c // 2 * 8 + c % 2 + 1, :]).astype(BF16)

    normed = jnp.concatenate([normed_columns(c) for c in range(2 * CHIPS)], axis=1)

    def hidden_units(gate, up):
        over = (((1,), (1,)), ((), ()))
        gate_out = lax.dot_general(normed, gate[...], over, preferred_element_type=F32)
        up_out = lax.dot_general(normed, up[...], over, preferred_element_type=F32)
        return (gate_out / (1.0 + jnp.exp(-gate_out)) * up_out).astype(BF16)

    act0, act1 = hidden_units(gate0, up0), hidden_units(gate1, up1)
    wide = 512
    for n in range(D // wide):
        place = slice(n * wide, (n + 1) * wide)
        partial = jnp.dot(act0, down0[:, place], preferred_element_type=F32) + jnp.dot(
            act1, down1[:, place], preferred_element_type=F32
        )
        for i in range(wide // HD):
            c = n * (wide // HD) + i
            sums[pl.ds(c, HALF, stride=2 * CHIPS), :] = partial[:, i * HD : (i + 1) * HD]
    message[...] = sums[...].astype(BF16)


def sum_kernel(parts, mid_row, out):
    chains = [parts[s].astype(F32) for s in range(8)]
    for s in range(8, CHIPS * TP):
        chains[s % 8] = chains[s % 8] + parts[s].astype(F32)
    while len(chains) > 1:
        chains = [x + y for x, y in zip(chains[::2], chains[1::2])]
    total = chains[0]
    total = (mid_row[...] + total).astype(BF16)
    for r in range(8):
        out[:, r * HD : (r + 1) * HD] = total[r : r + 1, :]


def in_vmem(shape, dtype):
    return pltpu.VMEM(shape, dtype)


def stay(x):
    return pltpu.with_memory_space_constraint(x, pltpu.HBM)


def held(x):
    return pltpu.with_memory_space_constraint(x, pltpu.VMEM)


def call(kernel, out_shape, operands, scratch=(), far=(), pinned=(), limit=SMALL, cost=None):
    vmem = pl.BlockSpec(memory_space=pltpu.VMEM)
    specs = [pl.BlockSpec(memory_space=pl.ANY) if i in far else vmem for i in range(len(operands))]
    return pl.pallas_call(
        kernel,
        out_shape=out_shape,
        in_specs=specs,
        out_specs=jax.tree.map(lambda _: vmem, out_shape, is_leaf=lambda x: not isinstance(x, tuple)),
        scratch_shapes=list(scratch),
        compiler_params=pltpu.CompilerParams(vmem_limit_bytes=limit),
        cost_estimate=cost,
    )(*(stay(x) if i in pinned else x for i, x in enumerate(operands)))


def shards(
    hidden_in,
    query,
    new_key,
    new_value,
    cache_keys,
    cache_values,
    lengths,
    out_weight,
    norm_gain,
    w_gate,
    w_up,
    w_down,
):
    def other_core(x):
        return lax.ppermute(x, "k", [(0, 1), (1, 0)])

    w_gate, w_up = w_gate.T, w_up.T
    inputs = (query, hidden_in, new_key, new_value, lengths)
    message, own, limits = call(
        start_kernel,
        (in_vmem((SEQS, 16, HD), BF16), in_vmem((2, HEADS, HD), F32), in_vmem((SEQS, HD), jnp.int32)),
        (*inputs, cache_keys, cache_values),
        [
            *(pltpu.VMEM(x.shape, x.dtype) for x in inputs[:4]),
            pltpu.SMEM(lengths.shape, jnp.int32),
            pltpu.SemaphoreType.DMA((5,)),
        ],
        far=range(7),
        pinned=range(7),
    )
    gathered = lax.all_to_all(message, ("p", "k"), 0, 0, tiled=True)
    *exchanged, gathered = lax.optimization_barrier((out_weight, w_gate, w_up, w_down, gathered))
    other_out_weight, other_gate, other_up, other_down = map(other_core, exchanged)
    cache = held(cache_keys), held(cache_values)
    sent = call(
        other_kernel,
        in_vmem((MSG, HD), BF16),
        (limits, gathered, *cache),
        [pltpu.VMEM((ROWS, HD), F32), pltpu.VMEM((ROWS, HD), F32)],
    )
    came = other_core(sent)
    kept, kept_lse, hidden_part = call(
        kept_kernel,
        (in_vmem((ROWS, HD), F32), in_vmem((ROWS, HD), F32), in_vmem((2, HALF, HD), F32)),
        (limits, gathered, own, *cache),
        [
            pltpu.VMEM((ROWS + HALF, HD), F32),
            pltpu.VMEM((ROWS + HALF, HD), F32),
            pltpu.VMEM((SEQS * 16 + 32, HD), F32),
        ],
    )
    blocks = call(merge_kernel, in_vmem((CHIPS, MSG, HD), BF16), (kept, kept_lse, came))
    blocks, other_gate, other_up, other_down, other_out_weight = lax.optimization_barrier(
        (blocks, other_gate, other_up, other_down, other_out_weight)
    )
    blocks = lax.all_to_all(blocks, "p", 0, 0, tiled=True)
    columns = call(
        project_kernel,
        in_vmem((CHIPS * TP, 2 * HALF + 8, HD), BF16),
        (blocks, hidden_part, norm_gain.reshape(8, HD), out_weight, other_out_weight),
    )
    columns = lax.all_to_all(columns, ("p", "t"), 0, 0, tiled=True)
    partial, mid_row = call(
        feed_kernel,
        (in_vmem((CHIPS * TP * 8, HD), BF16), in_vmem((8, HD), F32)),
        (columns, w_gate, w_up, other_gate, other_up, w_down, other_down),
        [
            pltpu.VMEM((2 * CHIPS * HALF + HALF, HD), F32),
            pltpu.VMEM((CHIPS * TP * 8, HD), F32),
            pltpu.VMEM((CHIPS * 8, HD), F32),
        ],
    )
    partial = lax.all_to_all(partial.reshape(CHIPS * TP, 8, HD), ("p", "t"), 0, 0, tiled=True)
    return call(sum_kernel, jax.ShapeDtypeStruct((1, 8 * HD), BF16), (partial, mid_row))


def solution(mesh):
    cut = Mesh(mesh.devices.reshape(CHIPS, 2, TP), ("p", "k", "t"))
    ctx, tp = ("p", "k"), "t"
    return jax.shard_map(
        shards,
        mesh=cut,
        in_specs=(
            P(ctx, tp),
            P(ctx, tp),
            P(ctx, tp),
            P(ctx, tp),
            P(None, ctx, tp),
            P(None, ctx, tp),
            P(),
            P(tp, ctx),
            P(tp),
            P(None, ("p", "k", "t")),
            P(None, ("p", "k", "t")),
            P(("p", "k", "t"), None),
        ),
        out_specs=P(ctx, tp),
        check_vma=False,
    )
```

```python
import functools
import math

import jax
import jax.numpy as jnp
from jax import lax
from jax.experimental import pallas as pl
from jax.experimental.pallas import tpu as pltpu
from jax.sharding import Mesh
from jax.sharding import PartitionSpec as P

D = 4096
HD = 128
EPSILON = 1e-05
MASKED = -1e30
F32 = jnp.float32
BF16 = jnp.bfloat16

CHIPS = 16
TP = 4
SEQS = 32
HALF = 16
HEADS = 8
GROUP = 8
ROWS = HEADS * HALF
MSG = ROWS + 8

SMALL = 8 * 1024 * 1024


def pack_lse(lse_of_head):
    lane = lax.broadcasted_iota(jnp.int32, (HALF, 128), 1)
    packed = jnp.zeros((HALF, 128), F32)
    for h in range(HEADS):
        for i, part in enumerate(addends(lse_of_head(h))):
            packed = jnp.where(lane == i * HEADS + h, part, packed)
    return (packed[:8] + pltpu.roll(packed[8:], 3 * HEADS, 1)).astype(BF16)


def unpack_lse(packed):
    packed = packed.astype(F32)
    packed = jnp.concatenate([packed, pltpu.roll(packed, 128 - 3 * HEADS, 1)], axis=0)
    return (packed + pltpu.roll(packed, 128 - HEADS, 1)) + pltpu.roll(packed, 128 - 2 * HEADS, 1)


def addends(x):
    high = x.astype(BF16).astype(F32)
    middle = (x - high).astype(BF16).astype(F32)
    return high, middle, x - high - middle


def copy_in(sources, targets, arrived):
    copies = [pltpu.make_async_copy(a, b, arrived.at[i]) for i, (a, b) in enumerate(zip(sources, targets))]
    for copy in copies:
        copy.start()
    return copies


def start_kernel(*refs):
    sources, (message, own, limits), landed, arrived = refs[:5], refs[7:10], refs[10:15], refs[15]
    copies = copy_in(sources, landed, arrived)
    for copy in copies[:2]:
        copy.wait()
    query, hidden, own_key, own_value, lengths = landed

    def rows(x):
        x = x[...].astype(F32)
        return jnp.concatenate([x[:, r * HD : (r + 1) * HD] for r in range(8)], axis=0)

    def heads(x):
        x = x[...].astype(F32)
        return jnp.concatenate([x[:, (h // 4) * HD : (h // 4 + 1) * HD] for h in range(HEADS)], axis=0)

    queries = rows(query)
    both = jnp.concatenate([queries, rows(hidden)], axis=0).astype(BF16)
    message[...] = jnp.broadcast_to(both[None], message.shape)
    for copy in copies[2:]:
        copy.wait()
    score = jnp.sum(queries * heads(own_key), axis=1, keepdims=True) * (1.0 / math.sqrt(HD))
    own[0] = jnp.broadcast_to(score, (HEADS, HD))
    own[1] = heads(own_value)
    for b in range(SEQS):
        limits[b : b + 1, :] = jnp.full((1, HD), lengths[b], jnp.int32)


def attend(parity, limits, gathered, keys, values, outs, lses):
    chip, core = lax.axis_index("p"), lax.axis_index("k")
    ctx_dev = keys.shape[1]
    factor = 1.0 / math.sqrt(HD)
    head = lax.broadcasted_iota(jnp.int32, (HEADS, HD), 0)
    zero = jnp.zeros((HEADS, HD), BF16)
    places = (chip * 2 + core) * ctx_dev + lax.broadcasted_iota(jnp.int32, (HEADS, ctx_dev), 1)

    def score(b):
        query = gathered[b][:HEADS]
        wide = jnp.concatenate(
            [jnp.where(head < HEADS // 2, query, zero), jnp.where(head >= HEADS // 2, query, zero)], axis=1
        )
        return lax.dot_general(wide, keys[b], (((1,), (1,)), ((), ())), preferred_element_type=F32) * factor

    def soften(b, scores):
        limit = limits[pl.ds(b, 1), :]
        valid = places < jnp.concatenate([limit] * (ctx_dev // HD), axis=1)
        top = jnp.max(jnp.where(valid, scores, MASKED), axis=1, keepdims=True)
        weights = jnp.where(valid, jnp.exp(scores - top), 0.0).astype(BF16)
        return top, weights, jnp.sum(weights.astype(F32), axis=1, keepdims=True)

    def collect(b, top, weights, den):
        num = jnp.dot(weights, values[b], preferred_element_type=F32)
        num = jnp.where(head < HEADS // 2, num[:, :HD], num[:, HD:])
        some = den > 0.0
        safe = jnp.where(some, den, 1.0)
        return num / safe, jnp.where(some, top + jnp.log(safe), MASKED)

    for at in range(0, HALF, GROUP):
        sequences = [2 * j + parity for j in range(at, at + GROUP)]
        scores = [score(b) for b in sequences]
        softened = [soften(b, x) for b, x in zip(sequences, scores)]
        collected = [collect(b, *x) for b, x in zip(sequences, softened)]
        for i, (out, lse) in enumerate(collected):
            outs[pl.ds(at + i, HEADS, stride=HALF), :] = out
            lses[pl.ds(at + i, HEADS, stride=HALF), :] = jnp.broadcast_to(lse, (HEADS, HD))


def other_kernel(limits, gathered, keys, values, sent, outs, lses):
    attend(1 - lax.axis_index("k"), limits, gathered, keys, values, outs, lses)
    sent[:ROWS, :] = outs[...].astype(BF16)
    sent[ROWS:, :] = pack_lse(lambda h: lses[h * HALF : (h + 1) * HALF, :])


def kept_kernel(limits, gathered, own, keys, values, kept, kept_lse, hidden_part, outs, lses, rows):
    chip, core, plane = lax.axis_index("p"), lax.axis_index("k"), lax.axis_index("t")
    attend(core, limits, gathered, keys, values, outs, lses)
    fresh_score, value = own[0], own[1]
    place = pl.ds(chip, HEADS, stride=HALF)
    cached, block_lse = outs[place, :], lses[place, :]
    top = jnp.maximum(block_lse, fresh_score)
    keep, fresh = jnp.exp(block_lse - top), jnp.exp(fresh_score - top)
    total = keep + fresh
    outs[place, :] = (cached * keep + value * fresh) / total
    lses[place, :] = top + jnp.log(total)
    kept[...] = outs[:ROWS, :]
    kept_lse[...] = lses[:ROWS, :]
    rows[: SEQS * 16, :] = gathered[...].reshape(SEQS * 16, HD).astype(F32)
    column = core * 16 + HEADS + (chip % 4) * 2
    for i in range(2):
        part = rows[pl.ds(column + i, HALF, stride=32), :]
        hidden_part[i] = jnp.where(plane == chip // 4, part, 0.0)


def merge_kernel(kept, kept_lse, came, message):
    came_lse = unpack_lse(came[ROWS:, :])
    merged_lse = []
    for h in range(HEADS):
        place = slice(h * HALF, (h + 1) * HALF)
        mine = kept_lse[place, :]
        theirs = came_lse[:, h : h + 1]
        top = jnp.maximum(mine, theirs)
        left, right = jnp.exp(mine - top), jnp.exp(theirs - top)
        total = left + right
        block = (kept[place, :] * left + came[place, :].astype(F32) * right) / total
        message[:, place, :] = jnp.broadcast_to(block.astype(BF16)[None], (CHIPS, HALF, HD))
        merged_lse.append(top + jnp.log(total))
    packed = pack_lse(lambda h: merged_lse[h])
    message[:, ROWS:, :] = jnp.broadcast_to(packed[None], (CHIPS, 8, HD))


def project_kernel(blocks, hidden_part, gain, weight, other_weight, message):
    chip, core, plane = lax.axis_index("p"), lax.axis_index("k"), lax.axis_index("t")
    lse = []
    for s in range(CHIPS):
        lse.append(unpack_lse(blocks[s, ROWS:, :]))
    top = lse[0]
    for s in range(1, CHIPS):
        top = jnp.maximum(top, lse[s])
    share = [jnp.exp(x - top) for x in lse]
    total = share[0]
    for s in range(1, CHIPS):
        total = total + share[s]
    share = [x / total for x in share]
    columns = []
    for h in range(HEADS):
        place = slice(h * HALF, (h + 1) * HALF)
        acc = jnp.zeros((HALF, HD), F32)
        for s in range(CHIPS):
            acc = acc + share[s][:, h : h + 1] * blocks[s, place, :].astype(F32)
        columns.append(acc.astype(BF16))
    attention = jnp.concatenate(columns, axis=1)
    mine = jnp.dot(attention, weight[...], preferred_element_type=F32)
    other = jnp.dot(attention, other_weight[...], preferred_element_type=F32)
    low, high = jnp.where(core == 0, mine, other), jnp.where(core == 0, other, mine)
    for i, rows in enumerate((low, high)):
        rows = (rows + hidden_part[i]).astype(BF16)
        message[:, i * HALF : (i + 1) * HALF, :] = jnp.broadcast_to(rows[None], (CHIPS * TP, HALF, HD))
    rows = jnp.concatenate([*addends(gain[pl.ds((chip % 4) * 2, 2), :]), jnp.zeros((2, HD), F32)], axis=0)
    rows = jnp.where(plane == chip // 4, rows, 0.0).astype(BF16)
    message[:, 2 * HALF :, :] = jnp.broadcast_to(rows[None], (CHIPS * TP, 8, HD))


def feed_kernel(
    parts, gate0, up0, gate1, up1, down0, down1, message, mid_row, mid, sums, gains
):
    chip, plane = lax.axis_index("p"), lax.axis_index("t")
    for c in range(CHIPS):
        rows = parts[c * TP + c // 4, 2 * HALF :, :].astype(F32)
        gains[c * 8 : (c + 1) * 8, :] = (rows + pltpu.roll(rows, 6, 0)) + pltpu.roll(rows, 4, 0)
    square = jnp.zeros((HALF, HD), F32)
    for c in range(2 * CHIPS):
        place = slice((c % 2) * HALF, (c % 2 + 1) * HALF)
        piece = parts[(c // 2) * TP, place, :].astype(F32)
        for t in range(1, TP):
            piece = piece + parts[(c // 2) * TP + t, place, :].astype(F32)
        mid[c * HALF : (c + 1) * HALF, :] = piece
        square = square + piece * piece
    scale = lax.rsqrt(jnp.sum(square, axis=1, keepdims=True) / D + EPSILON)
    mid_row[...] = mid[pl.ds(plane * 8 * HALF + chip, 8, stride=HALF), :]

    def normed_columns(c):
        return (mid[c * HALF : (c + 1) * HALF, :] * scale * gains[c // 2 * 8 + c % 2 : c // 2 * 8 + c % 2 + 1, :]).astype(BF16)

    normed = jnp.concatenate([normed_columns(c) for c in range(2 * CHIPS)], axis=1)

    def hidden_units(gate, up):
        over = (((1,), (1,)), ((), ()))
        gate_out = lax.dot_general(normed, gate[...], over, preferred_element_type=F32)
        up_out = lax.dot_general(normed, up[...], over, preferred_element_type=F32)
        return (gate_out / (1.0 + jnp.exp(-gate_out)) * up_out).astype(BF16)

    act0, act1 = hidden_units(gate0, up0), hidden_units(gate1, up1)
    wide = 512
    for n in range(D // wide):
        place = slice(n * wide, (n + 1) * wide)
        partial = jnp.dot(act0, down0[:, place], preferred_element_type=F32) + jnp.dot(
            act1, down1[:, place], preferred_element_type=F32
        )
        for i in range(wide // HD):
            c = n * (wide // HD) + i
            sums[pl.ds(c, HALF, stride=2 * CHIPS), :] = partial[:, i * HD : (i + 1) * HD]
    message[...] = sums[...].astype(BF16)


def sum_kernel(parts, mid_row, out):
    total = parts[0].astype(F32)
    for s in range(1, CHIPS * TP):
        total = total + parts[s].astype(F32)
    total = (mid_row[...] + total).astype(BF16)
    for r in range(8):
        out[:, r * HD : (r + 1) * HD] = total[r : r + 1, :]


def in_vmem(shape, dtype):
    return pltpu.VMEM(shape, dtype)


def stay(x):
    return pltpu.with_memory_space_constraint(x, pltpu.HBM)


def held(x):
    return pltpu.with_memory_space_constraint(x, pltpu.VMEM)


def call(kernel, out_shape, operands, scratch=(), far=(), pinned=(), limit=SMALL, cost=None):
    vmem = pl.BlockSpec(memory_space=pltpu.VMEM)
    specs = [pl.BlockSpec(memory_space=pl.ANY) if i in far else vmem for i in range(len(operands))]
    return pl.pallas_call(
        kernel,
        out_shape=out_shape,
        in_specs=specs,
        out_specs=jax.tree.map(lambda _: vmem, out_shape, is_leaf=lambda x: not isinstance(x, tuple)),
        scratch_shapes=list(scratch),
        compiler_params=pltpu.CompilerParams(vmem_limit_bytes=limit),
        cost_estimate=cost,
    )(*(stay(x) if i in pinned else x for i, x in enumerate(operands)))


def shards(
    hidden_in,
    query,
    new_key,
    new_value,
    cache_keys,
    cache_values,
    lengths,
    out_weight,
    norm_gain,
    w_gate,
    w_up,
    w_down,
):
    def other_core(x):
        return lax.ppermute(x, "k", [(0, 1), (1, 0)])

    w_gate, w_up = w_gate.T, w_up.T
    inputs = (query, hidden_in, new_key, new_value, lengths)
    message, own, limits = call(
        start_kernel,
        (in_vmem((SEQS, 16, HD), BF16), in_vmem((2, HEADS, HD), F32), in_vmem((SEQS, HD), jnp.int32)),
        (*inputs, cache_keys, cache_values),
        [
            *(pltpu.VMEM(x.shape, x.dtype) for x in inputs[:4]),
            pltpu.SMEM(lengths.shape, jnp.int32),
            pltpu.SemaphoreType.DMA((5,)),
        ],
        far=range(7),
        pinned=range(7),
    )
    gathered = lax.all_to_all(message, ("p", "k"), 0, 0, tiled=True)
    *exchanged, gathered = lax.optimization_barrier((out_weight, w_gate, w_up, w_down, gathered))
    other_out_weight, other_gate, other_up, other_down = map(other_core, exchanged)
    cache = held(cache_keys), held(cache_values)
    sent = call(
        other_kernel,
        in_vmem((MSG, HD), BF16),
        (limits, gathered, *cache),
        [pltpu.VMEM((ROWS, HD), F32), pltpu.VMEM((ROWS, HD), F32)],
    )
    came = other_core(sent)
    kept, kept_lse, hidden_part = call(
        kept_kernel,
        (in_vmem((ROWS, HD), F32), in_vmem((ROWS, HD), F32), in_vmem((2, HALF, HD), F32)),
        (limits, gathered, own, *cache),
        [
            pltpu.VMEM((ROWS + HALF, HD), F32),
            pltpu.VMEM((ROWS + HALF, HD), F32),
            pltpu.VMEM((SEQS * 16 + 32, HD), F32),
        ],
    )
    blocks = call(merge_kernel, in_vmem((CHIPS, MSG, HD), BF16), (kept, kept_lse, came))
    blocks, other_gate, other_up, other_down, other_out_weight = lax.optimization_barrier(
        (blocks, other_gate, other_up, other_down, other_out_weight)
    )
    blocks = lax.all_to_all(blocks, "p", 0, 0, tiled=True)
    columns = call(
        project_kernel,
        in_vmem((CHIPS * TP, 2 * HALF + 8, HD), BF16),
        (blocks, hidden_part, norm_gain.reshape(8, HD), out_weight, other_out_weight),
    )
    columns = lax.all_to_all(columns, ("p", "t"), 0, 0, tiled=True)
    partial, mid_row = call(
        feed_kernel,
        (in_vmem((CHIPS * TP * 8, HD), BF16), in_vmem((8, HD), F32)),
        (columns, w_gate, w_up, other_gate, other_up, w_down, other_down),
        [
            pltpu.VMEM((2 * CHIPS * HALF + HALF, HD), F32),
            pltpu.VMEM((CHIPS * TP * 8, HD), F32),
            pltpu.VMEM((CHIPS * 8, HD), F32),
        ],
    )
    partial = lax.all_to_all(partial.reshape(CHIPS * TP, 8, HD), ("p", "t"), 0, 0, tiled=True)
    return call(sum_kernel, jax.ShapeDtypeStruct((1, 8 * HD), BF16), (partial, mid_row))


def solution(mesh):
    cut = Mesh(mesh.devices.reshape(CHIPS, 2, TP), ("p", "k", "t"))
    ctx, tp = ("p", "k"), "t"
    return jax.shard_map(
        shards,
        mesh=cut,
        in_specs=(
            P(ctx, tp),
            P(ctx, tp),
            P(ctx, tp),
            P(ctx, tp),
            P(None, ctx, tp),
            P(None, ctx, tp),
            P(),
            P(tp, ctx),
            P(tp),
            P(None, ("p", "k", "t")),
            P(None, ("p", "k", "t")),
            P(("p", "k", "t"), None),
        ),
        out_specs=P(ctx, tp),
        check_vma=False,
    )
```
